256 devices in a mesh: stream: 32 (over x, z), azim: 8 (over y, core).
Axes of the slice: x: 4, y: 4, z: 8, core: 2. Of those that a mesh axis runs over, the one named last changes fastest.
Arguments:
- species_mass_density: float32 [14, 256, 32, 1024], P(None, 'stream', None, 'azim'), may hold values from -6 to 6
- axial_speed: float32 [256, 32, 1024], P('stream', None, 'azim'), may hold values from -6 to 6
- circumferential_speed: float32 [256, 32, 1024], P('stream', None, 'azim'), may hold values from -6 to 6
- thermal_kelvin_field: float32 [256, 32, 1024], P('stream', None, 'azim'), may hold values from 1 to 4
- arrhenius_multiplier: float32 [32], replicated, may hold values from 0.8 to 810
- arrhenius_threshold: float32 [32], replicated, may hold values from 2 to 24
- consumed_species_orders: float32 [32, 14], replicated, may hold values from -1.5 to 1.5
- net_molar_change: float32 [14, 32], replicated, may hold values from -1 to 1
- ablated_mixture_table: float32 [14, 14], replicated, may hold values from -1.5 to 1.5
- ablator_boundary_condition: float32 [8192, 14, 1024], P('stream', None, 'azim'), may hold values from -6 to 6
- holding_segment: int32 [8192], P('stream'), may hold values from 0 to 31, as said below
- intra_segment_position: int32 [8192], P('stream'), may hold values from 0 to 7
- shocked_level_bounds: int32 [32, 2], P('stream'), may hold values from 0 to 32, as said below
Outputs:
- rhs: float32 [14, 256, 32, 1024], P(None, 'stream', None, 'azim')
The draws below stay inside these ranges and needn't reach their ends.
Inputs may be any that keep to these rules, and one draw needn't show every extreme that they name: `holding_segment`: in each aligned block of 256 entries no tile appears more than 16 times, and some tile appears exactly 16 times in every block. Each row holds 0 <= shocked_level_bounds[t, 0] < shocked_level_bounds[t, 1] <= 32 with shocked_level_bounds[t, 1] - shocked_level_bounds[t, 0] <= 8; some row has exactly 8.
All inputs are finite; a program needn't handle non-finite values.
Results may differ from the reference program's by a relative error of at most 0.0003.
Values sent between devices are 32-bit elements; how exact they have to be, the bound alone decides.
A program may use at most 128 MiB of HBM per device.

```python
import math
import jax
import jax.numpy as jnp
from jax import lax

NSP = 14
MODES = 512
REACT = 32
SEGMENT_SPAN = 8
DEPTH_LEVELS = 32
ELEM_DEV = 256
ANGULAR_SAMPLES = 1024
TILES = 32
AXIAL_SLOTS = 256
ELEMS = 8192
CAP = 16
BAND = 8


def arrhenius_pair(key):
    key_energy, key_spread = jax.random.split(jax.random.fold_in(key, 71))
    log_energy = jax.random.uniform(key_energy, (REACT,), jnp.float32, math.log(2.0), math.log(24.0))
    threshold = jnp.exp(log_energy)
    log_spread = jax.random.uniform(key_spread, (REACT,), jnp.float32, math.log(0.5), math.log(2.0))
    multiplier = jnp.exp(log_spread) * jnp.exp(threshold * 0.25)
    return (multiplier, threshold)


def draw_arrhenius_multiplier(key, part):
    paired = arrhenius_pair(key)
    return paired[0].astype(jnp.float32)


def draw_arrhenius_threshold(key, part):
    paired = arrhenius_pair(key)
    return paired[1].astype(jnp.float32)


def draw_holding_segment(key, part):
    key = jax.random.fold_in(key, 11)
    key_special, key_rest = jax.random.split(key)
    special = jax.random.randint(key_special, (), 0, TILES)

    def one_block(subkey):
        key_slots, key_order = jax.random.split(subkey)
        free_slots = jax.random.permutation(key_slots, (TILES - 1) * CAP)[:ELEM_DEV - CAP]
        others = free_slots // CAP
        others = jnp.where(others >= special, others + 1, others)
        picks = jnp.concatenate([jnp.full((CAP,), special, jnp.int32), others.astype(jnp.int32)])
        return jax.random.permutation(key_order, picks)
    blocks = jax.vmap(one_block)(jax.random.split(key_rest, TILES))
    return blocks.reshape(-1).astype(jnp.int32)


def draw_shocked_level_bounds(key, part):
    key = jax.random.fold_in(key, 23)
    key_width, key_widest, key_low = jax.random.split(key, 3)
    widths = jax.random.randint(key_width, (TILES,), max(1, BAND // 4), BAND + 1)
    widest = jax.random.randint(key_widest, (), 0, TILES)
    widths = jnp.where(jnp.arange(TILES) == widest, BAND, widths)
    lows = jax.random.randint(key_low, (TILES,), 0, DEPTH_LEVELS + 1) % (DEPTH_LEVELS - widths + 1)
    return jnp.stack([lows, lows + widths], axis=1).astype(jnp.int32)


def set_ends(array, key, low, largest):
    place = [jax.random.randint(jax.random.fold_in(key, axis), (), 0, length) for axis, length in enumerate(array.shape)]
    main_axis = array.shape.index(max(array.shape))
    next_to = place[:main_axis] + [(place[main_axis] + 1) % array.shape[main_axis]] + place[main_axis + 1:]
    return array.at[tuple(place)].set(low).at[tuple(next_to)].set(largest)


def shard_levels(stream_key, shape, shards, smallest, top_value):
    def one(position, blocks):
        heights = jax.random.uniform(jax.random.fold_in(jax.random.fold_in(stream_key, 6), position), (blocks,), jnp.float32, smallest / len(shards), top_value / len(shards))
        return jnp.repeat(jnp.exp(heights), shape[position] // blocks).reshape((-1,) + (1,) * (len(shape) - position - 1))

    factor_of = one(*shards[0])
    for cut in shards[1:]:
        factor_of = factor_of * one(*cut)
    return factor_of


def gaussian(stream_key, extent, spread, bound, pieces=(), dtype=jnp.bfloat16):
    array = jax.random.normal(stream_key, extent, jnp.float32) * spread
    if len(pieces) > 0:
        array = shard_levels(stream_key, extent, pieces, -0.22, 0.18) * array
    return jnp.clip(array, min=-bound, max=bound).astype(dtype)


def setup_inputs(seed: int = 0) -> dict:
    arg_keys = jax.random.split(jax.random.key(seed), 14)
    return {
        "species_mass_density": gaussian(arg_keys[0], (NSP, AXIAL_SLOTS, DEPTH_LEVELS, ANGULAR_SAMPLES), 1.0, 6.0, ((1, 32), (3, 8)), jnp.float32),
        "axial_speed": gaussian(arg_keys[1], (AXIAL_SLOTS, DEPTH_LEVELS, ANGULAR_SAMPLES), 1.0, 6.0, ((0, 32), (2, 8)), jnp.float32),
        "circumferential_speed": gaussian(arg_keys[2], (AXIAL_SLOTS, DEPTH_LEVELS, ANGULAR_SAMPLES), 1.0, 6.0, ((0, 32), (2, 8)), jnp.float32),
        "thermal_kelvin_field": jnp.clip(1.0 + 3.0 * jax.random.uniform(arg_keys[3], (AXIAL_SLOTS, DEPTH_LEVELS, ANGULAR_SAMPLES), jnp.float32) ** shard_levels(arg_keys[3], (AXIAL_SLOTS, DEPTH_LEVELS, ANGULAR_SAMPLES), ((0, 32), (2, 8)), -0.2, 0.2), 1.0, 4.0),
        "arrhenius_multiplier": draw_arrhenius_multiplier(jax.random.fold_in(arg_keys[13], 71), 0),
        "arrhenius_threshold": draw_arrhenius_threshold(jax.random.fold_in(arg_keys[13], 71), 0),
        "consumed_species_orders": gaussian(arg_keys[6], (REACT, NSP), NSP ** -0.5, 1.5, (), jnp.float32),
        "net_molar_change": gaussian(arg_keys[7], (NSP, REACT), REACT ** -0.5, 1.0, (), jnp.float32),
        "ablated_mixture_table": gaussian(arg_keys[8], (NSP, NSP), NSP ** -0.5, 1.5, (), jnp.float32),
        "ablator_boundary_condition": gaussian(arg_keys[9], (ELEMS, NSP, ANGULAR_SAMPLES), 1.0, 6.0, ((0, 32), (2, 8)), jnp.float32),
        "holding_segment": draw_holding_segment(jax.random.fold_in(arg_keys[13], 71), 0),
        "intra_segment_position": set_ends(jax.random.randint(arg_keys[11], (ELEMS,), 0, SEGMENT_SPAN), jax.random.fold_in(arg_keys[11], 1), 0, SEGMENT_SPAN - 1).astype(jnp.int32),
        "shocked_level_bounds": draw_shocked_level_bounds(jax.random.fold_in(arg_keys[13], 71), 0),
    }


STENCIL = (-1.0 / 60.0, 3.0 / 20.0, -0.75, 0.0, 0.75, -3.0 / 20.0, 1.0 / 60.0)
HIGH = lax.Precision.HIGHEST


def reference(species_mass_density, axial_speed, circumferential_speed, thermal_kelvin_field, arrhenius_multiplier, arrhenius_threshold, consumed_species_orders, net_molar_change, ablated_mixture_table, ablator_boundary_condition, holding_segment, intra_segment_position, shocked_level_bounds):
    flux = jnp.einsum("st,etj->esj", ablated_mixture_table, ablator_boundary_condition, precision=HIGH)
    target = (holding_segment * SEGMENT_SPAN + intra_segment_position).astype(jnp.int32)
    wall_all = jax.ops.segment_sum(flux, target, num_segments=AXIAL_SLOTS)
    padded = jnp.pad(species_mass_density, ((0, 0), (3, 3), (0, 0), (0, 0)))
    wave_int = jnp.arange(MODES + 1).astype(jnp.int32)
    wave = wave_int.astype(jnp.float32)
    sigma = (3 * wave_int < 2 * MODES).astype(jnp.float32)
    factor = 1j * wave * sigma / MODES
    row_index = jnp.arange(DEPTH_LEVELS).astype(jnp.int32)

    def one_tile(tile):
        leading_position = (tile * SEGMENT_SPAN).astype(jnp.int32)
        block = lax.dynamic_slice_in_dim(padded, leading_position, SEGMENT_SPAN + 6, 1)
        own = block[:, 3:3 + SEGMENT_SPAN]
        stream_grad = STENCIL[0] * block[:, 0:SEGMENT_SPAN]
        for offset in range(1, 7):
            if STENCIL[offset] != 0.0:
                stream_grad = stream_grad + STENCIL[offset] * block[:, offset:offset + SEGMENT_SPAN]
        spectrum = jnp.fft.rfft(own, axis=-1)
        azim_grad = jnp.fft.irfft(spectrum * factor, n=ANGULAR_SAMPLES, axis=-1)
        in_band = ((row_index >= shocked_level_bounds[tile, 0]) & (row_index < shocked_level_bounds[tile, 1])).astype(jnp.float32)
        velocity = lax.dynamic_slice_in_dim(axial_speed, leading_position, SEGMENT_SPAN, 0)
        swirl = lax.dynamic_slice_in_dim(circumferential_speed, leading_position, SEGMENT_SPAN, 0)
        enthalpy_liberated = lax.dynamic_slice_in_dim(thermal_kelvin_field, leading_position, SEGMENT_SPAN, 0)
        mixed = jnp.einsum("rs,sxya->rxya", consumed_species_orders, own, precision=HIGH)
        rate = arrhenius_multiplier[:, None, None, None] * jnp.exp(-arrhenius_threshold[:, None, None, None] / enthalpy_liberated[None])
        chem = jnp.einsum("sr,rxya->sxya", net_molar_change, rate * mixed, precision=HIGH)
        rhs = -velocity[None] * stream_grad - swirl[None] * in_band[None, None, :, None] * azim_grad + chem
        wall = jnp.transpose(lax.dynamic_slice_in_dim(wall_all, leading_position, SEGMENT_SPAN, 0), (1, 0, 2))
        return rhs.at[:, :, 0, :].add(wall)

    tiles_out = lax.map(one_tile, jnp.arange(TILES).astype(jnp.int32))
    return jnp.transpose(tiles_out, (1, 0, 2, 3, 4)).reshape(NSP, AXIAL_SLOTS, DEPTH_LEVELS, ANGULAR_SAMPLES)
```

```python
import functools
import math

import jax
import jax.numpy as jnp
import numpy as np
from jax import lax
from jax.experimental import pallas as pl
from jax.experimental.pallas import tpu as pltpu
from jax.sharding import PartitionSpec as P

STENCIL = (-1.0 / 60.0, 3.0 / 20.0, -0.75, 0.0, 0.75, -3.0 / 20.0, 1.0 / 60.0)
MESH = pl.DeviceIdType.MESH
HIGH = lax.Precision.HIGHEST
BF, F32 = jnp.bfloat16, jnp.float32

SP, CELLS, ROWS, PTS = 14, 8, 32, 128
REACT, ELEMS, BAND, GROUPS = 32, 256, 8, 8
NX, NZ, TILES = 4, 8, 32
PAD = ROWS - BAND
HALF = 16
CHUNKS = (((0, 4), (4, 8)), ((8, 11), (11, 14)))


def derivative_strip():
    points, modes = PTS * GROUPS, PTS * GROUPS // 2
    wave = np.arange(modes, dtype=np.float64)
    gain = np.where(3 * np.arange(modes) < 2 * modes, wave, 0.0)
    lag = np.arange(points)
    phase = (lag[:, None] * np.arange(modes)[None, :]) % points
    d = -2.0 / (points * modes) * (np.sin(phase * (2.0 * np.pi / points)) @ gain)
    strip = d[(lag[None, :] - np.arange(2 * PTS)[:, None]) % points].astype(np.float32)
    high = strip.astype(BF)
    low = (strip - high.astype(np.float32)).astype(BF)
    return high, low


def split(v):
    high = v.astype(BF)
    return high, (v - high.astype(F32)).astype(BF)


def dot(a, b):
    return jnp.dot(a, b, preferred_element_type=F32)


def dot3(ah, al, bh, bl):
    return dot(ah, bh) + dot(al, bh) + dot(ah, bl)


def spread(table, rows, cols):
    n, m = rows * HALF, cols * HALF
    left = (lax.broadcasted_iota(jnp.int32, (n, rows), 0) // HALF == lax.broadcasted_iota(jnp.int32, (n, rows), 1)).astype(F32).astype(BF)
    right = (lax.broadcasted_iota(jnp.int32, (cols, m), 1) // HALF == lax.broadcasted_iota(jnp.int32, (cols, m), 0)).astype(F32).astype(BF)
    same = lax.broadcasted_iota(jnp.int32, (n, m), 0) % HALF == lax.broadcasted_iota(jnp.int32, (n, m), 1) % HALF
    parts = []
    for part in split(table):
        wide = dot(dot(left, part).astype(BF), right)
        parts.append(jnp.where(same, wide, 0.0).astype(BF))
    return parts


def kernel(
    dens, axial, swirl, temp, mult, thr, cmat, nmat, tab, abl, seg, pos, bounds, strip_h, strip_l,
    out,
    dens_v, axial_v, swirl_v, temp_v, abl_v, sh_v, sl_v, kch, kcl, knh, knl, w, m3r, m3l, xr1, xl1, xal, xar, y, zr,
    fs, fr, gs, zb, halo_l, halo_r, v_wall, loc, ss, rs,
):
    s = lax.axis_index("stream")
    a = lax.axis_index("azim")
    x, z = s // NZ, lax.rem(s, NZ)
    up, down = lax.rem(s + 1, TILES), lax.rem(s + TILES - 1, TILES)
    xr, xl, xo = lax.rem(x + 1, NX), lax.rem(x + NX - 1, NX), lax.rem(x + 2, NX)
    right, left = (xr * NZ + z, a), (xl * NZ + z, a)
    y_peer = [lax.rem(a + d, GROUPS) for d in range(1, GROUPS)]
    z_peer = [lax.rem(z + d, NZ) for d in range(1, NZ)]

    barrier = pltpu.get_barrier_semaphore()
    peers = [(up, a), (down, a), right, left]
    peers += [(s, p) for p in y_peer] + [(x * NZ + p, a) for p in z_peer]
    for p in peers:
        pl.semaphore_signal(barrier, inc=1, device_id=p, device_id_type=MESH)

    local = []
    for src, dst in (
        (abl, abl_v), (dens, dens_v), (temp, temp_v), (axial, axial_v), (swirl, swirl_v),
        (strip_h, sh_v), (strip_l, sl_v),
    ):
        c = pltpu.make_async_copy(src, dst, loc.at[len(local)])
        c.start()
        local.append(c)

    count = [0]

    def remote(src, dst, device):
        n = count[0]
        count[0] += 1
        return pltpu.make_async_remote_copy(
            src_ref=src, dst_ref=dst, send_sem=ss.at[n], recv_sem=rs.at[n], device_id=device, device_id_type=MESH
        )

    target = seg[...] * CELLS + pos[...]
    place = (lax.broadcasted_iota(jnp.int32, (TILES * CELLS, ELEMS), 0) == target).astype(F32).astype(BF)
    local[0].wait()
    for p in range(SP // 2):
        block = jnp.concatenate([abl_v[2 * p], abl_v[2 * p + 1]], axis=1)
        high, low = split(block)
        sums = dot(place, high) + dot(place, low)
        w[2 * p] = sums[:, :PTS]
        w[2 * p + 1] = sums[:, PTS:]

    local[1].wait()
    start = jnp.minimum(bounds[0, 0], PAD)

    def gather(i, carry):
        for c in range(CELLS):
            fs[c, i] = dens_v[i, c, pl.ds(start, BAND), :]
        return carry

    lax.fori_loop(0, SP, gather, 0)
    pl.semaphore_wait(barrier, len(peers))

    def rows_of(block):
        return pl.ds(pl.multiple_of(block * NZ * CELLS, NZ * CELLS), NZ * CELLS)

    first, early, late = [], [], []
    for (r0, r1), (l0, l1) in CHUNKS:
        R, L = slice(r0, r1), slice(l0, l1)
        first.append([
            remote(w.at[R, rows_of(xo)], xr1.at[R], right),
            remote(w.at[L, rows_of(xo)], xl1.at[L], left),
        ])
        early.append([
            remote(w.at[L, rows_of(xr)], xal.at[L], right),
            remote(w.at[R, rows_of(xl)], xar.at[R], left),
        ])
        late.append([
            remote(m3r.at[R], xal.at[R], right),
            remote(m3l.at[L], xar.at[L], left),
        ])
    there, back = [], []
    for d in range(GROUPS - 1):
        there.append(remote(fs.at[y_peer[d]], fr.at[a], (s, y_peer[d])))
        back.append(remote(gs.at[y_peer[d]], zb.at[:, a, pl.ds(PAD, BAND)], (s, y_peer[d])))
    halo_up = remote(dens.at[:, CELLS - 3 : CELLS], halo_l, (up, a))
    halo_down = remote(dens.at[:, 0:3], halo_r, (down, a))
    z_sends = []
    for (r0, _), (_, l1) in CHUNKS:
        F = slice(r0, l1)
        z_sends.append([
            remote(y.at[F, pl.ds(pl.multiple_of(z_peer[d] * CELLS, CELLS), CELLS)], zr.at[d, F], (x * NZ + z_peer[d], a))
            for d in range(NZ - 1)
        ])

    for c in first[0] + early[0] + there:
        c.start()

    @pl.when(s < TILES - 1)
    def _():
        halo_up.start()

    @pl.when(s > 0)
    def _():
        halo_down.start()

    for c in first[1] + early[1]:
        c.start()

    fr[a] = fs[a]

    @pl.when(s == 0)
    def _():
        halo_l[...] = jnp.zeros_like(halo_l)

    @pl.when(s == TILES - 1)
    def _():
        halo_r[...] = jnp.zeros_like(halo_r)

    kch[...], kcl[...] = spread(jnp.transpose(cmat[...]), REACT, SP)
    knh[...], knl[...] = spread(nmat[...], SP, REACT)
    for c in local[2:]:
        c.wait()

    row = lax.broadcasted_iota(jnp.int32, (CELLS, ROWS, PTS), 1)
    in_band = (row >= bounds[0, 0]) & (row < bounds[0, 1])
    swirl_v[...] = jnp.where(in_band, swirl_v[...], 0.0)

    def clear(i, carry):
        zb[i, :, 0:PAD] = jnp.zeros((CELLS, PAD, PTS), F32)
        zb[i, :, PAD + BAND :] = jnp.zeros((CELLS, PAD, PTS), F32)
        return carry

    lax.fori_loop(0, SP, clear, 0)

    def chem(c, carry):
        block = dens_v[:, c]
        pair = jnp.concatenate(
            [block[:, :HALF].reshape(SP * HALF, PTS), block[:, HALF:].reshape(SP * HALF, PTS)], axis=1
        )
        high, low = split(pair)
        mixed = dot3(kch[...], kcl[...], high, low)
        minus = (-1.0 / math.log(2.0)) / temp_v[c]
        minus = jnp.concatenate([minus[:HALF], minus[HALF:]], axis=1)
        rate = jnp.concatenate([mult[q] * jnp.exp2(thr[q] * minus) for q in range(REACT)], axis=0)
        high, low = split(rate * mixed)
        made = dot3(knh[...], knl[...], high, low)
        out[:, c, 0:HALF] = made[:, :PTS].reshape(SP, HALF, PTS)
        out[:, c, HALF:] = made[:, PTS:].reshape(SP, HALF, PTS)
        return carry

    lax.fori_loop(0, 3, chem, 0)

    for k, ((r0, r1), (l0, l1)) in enumerate(CHUNKS):
        R, L = slice(r0, r1), slice(l0, l1)
        first[k][0].wait_recv()
        m3r[R] = w[R, rows_of(xr)] + xr1[R]
        late[k][0].start()
        first[k][1].wait_recv()
        m3l[L] = w[L, rows_of(xl)] + xl1[L]
        late[k][1].start()

    for c in there:
        c.wait_recv()
    lhs = jnp.concatenate(
        [
            jnp.concatenate([fr[2 * p].reshape(SP * BAND, PTS), fr[2 * p + 1].reshape(SP * BAND, PTS)], axis=1)
            for p in range(GROUPS // 2)
        ],
        axis=0,
    )
    high, low = split(lhs)
    n = SP * BAND
    shifted = [
        dot3(high, low, sh_v[:, 2 * PTS * c : 2 * PTS * (c + 1)], sl_v[:, 2 * PTS * c : 2 * PTS * (c + 1)])
        for c in range(GROUPS // 2)
    ]
    for q in range(GROUPS // 2):
        total = sum(shifted[(q - p) % 4][n * p : n * (p + 1)] for p in range(GROUPS // 2))
        gs[2 * q] = total[:, :PTS].reshape(SP, BAND, PTS)
        gs[2 * q + 1] = total[:, PTS:].reshape(SP, BAND, PTS)
    for c in back:
        c.start()
    zb[:, a, PAD : PAD + BAND] = gs[a]

    lax.fori_loop(3, 6, chem, 0)

    def finish_x(k):
        (r0, _), (_, l1) = CHUNKS[k]
        F = slice(r0, l1)
        for c in early[k] + late[k]:
            c.wait_recv()
        y[F] = w[F, rows_of(x)] + xal[F] + xar[F]
        for c in z_sends[k]:
            c.start()

    finish_x(0)
    lax.fori_loop(6, 8, chem, 0)
    finish_x(1)

    for c in back:
        c.wait_recv()

    def own(i, carry):
        f = dens_v[i]
        for c in range(CELLS):
            acc = None
            for j in (1, 2, 3):
                lo, hi = c - j >= 0, c + j < CELLS
                if lo and hi:
                    term = STENCIL[3 + j] * (f[c + j] - f[c - j])
                elif hi:
                    term = STENCIL[3 + j] * f[c + j]
                elif lo:
                    term = STENCIL[3 - j] * f[c - j]
                else:
                    continue
                acc = term if acc is None else acc + term
            around = zb[i, c, pl.ds(PAD - start, ROWS), :]
            out[i, c] = out[i, c] - axial_v[c] * acc - swirl_v[c] * around
        return carry

    lax.fori_loop(0, SP, own, 0)

    @pl.when(s > 0)
    def _():
        halo_up.wait_recv()

    @pl.when(s < TILES - 1)
    def _():
        halo_down.wait_recv()

    def ends(i, carry):
        before, after = halo_l[i], halo_r[i]
        for c in range(3):
            acc = sum(STENCIL[3 + j] * before[3 + c + j] for j in range(-3, -c))
            out[i, c] = out[i, c] - axial_v[c] * acc
            e = CELLS - 1 - c
            acc = sum(STENCIL[3 + j] * after[j - 1 - c] for j in range(c + 1, 4))
            out[i, e] = out[i, e] - axial_v[e] * acc
        return carry

    lax.fori_loop(0, SP, ends, 0)

    for k in range(len(CHUNKS)):
        for c in z_sends[k]:
            c.wait_recv()
    mine = pl.ds(pl.multiple_of(z * CELLS, CELLS), CELLS)
    for i in range(SP):
        v_wall[i] = y[i, mine] + sum(zr[d, i] for d in range(NZ - 1))
    for i in range(SP):
        wall = sum(tab[i, j] * v_wall[j] for j in range(SP))
        for c in range(CELLS):
            out[i, c, 0:1] = out[i, c, 0:1] + wall[c : c + 1]

    @pl.when(s < TILES - 1)
    def _():
        halo_up.wait_send()

    @pl.when(s > 0)
    def _():
        halo_down.wait_send()

    for group in first + early + late + z_sends + [there, back]:
        for c in group:
            c.wait_send()


def local(
    species_mass_density,
    axial_speed,
    circumferential_speed,
    thermal_kelvin_field,
    arrhenius_multiplier,
    arrhenius_threshold,
    consumed_species_orders,
    net_molar_change,
    ablated_mixture_table,
    ablator_boundary_condition,
    holding_segment,
    intra_segment_position,
    shocked_level_bounds,
):
    strip_h, strip_l = derivative_strip()
    far = pl.BlockSpec(memory_space=pltpu.HBM)
    near = pl.BlockSpec(memory_space=pltpu.VMEM)
    scalar = pl.BlockSpec(memory_space=pltpu.SMEM)
    vm = lambda shape, dtype=F32: pltpu.VMEM(shape, dtype)
    wide = NZ * CELLS
    copies = 6 * len(CHUNKS) + 2 * (GROUPS - 1) + 2 + len(CHUNKS) * (NZ - 1)
    return pl.pallas_call(
        kernel,
        name="section",
        out_shape=jax.ShapeDtypeStruct((SP, CELLS, ROWS, PTS), F32),
        in_specs=[far, far, far, far, scalar, scalar, near, near, scalar, far, near, near, scalar, far, far],
        out_specs=near,
        scratch_shapes=[
            vm((SP, CELLS, ROWS, PTS)), vm((CELLS, ROWS, PTS)), vm((CELLS, ROWS, PTS)), vm((CELLS, ROWS, PTS)),
            vm((SP, ELEMS, PTS)), vm((2 * PTS, GROUPS * PTS), BF), vm((2 * PTS, GROUPS * PTS), BF),
            vm((REACT * HALF, SP * HALF), BF), vm((REACT * HALF, SP * HALF), BF),
            vm((SP * HALF, REACT * HALF), BF), vm((SP * HALF, REACT * HALF), BF),
            vm((SP, TILES * CELLS, PTS)), vm((SP, wide, PTS)), vm((SP, wide, PTS)), vm((SP, wide, PTS)), vm((SP, wide, PTS)),
            vm((SP, wide, PTS)), vm((SP, wide, PTS)), vm((SP, wide, PTS)), vm((NZ - 1, SP, CELLS, PTS)),
            vm((GROUPS, SP, BAND, PTS)), vm((GROUPS, SP, BAND, PTS)), vm((GROUPS, SP, BAND, PTS)),
            vm((SP, CELLS, PAD + BAND + PAD, PTS)), vm((SP, 3, ROWS, PTS)), vm((SP, 3, ROWS, PTS)), vm((SP, CELLS, PTS)),
            pltpu.SemaphoreType.DMA((7,)), pltpu.SemaphoreType.DMA((copies,)), pltpu.SemaphoreType.DMA((copies,)),
        ],
        compiler_params=pltpu.CompilerParams(collective_id=0, has_side_effects=True, vmem_limit_bytes=56 << 20),
    )(
        species_mass_density, axial_speed, circumferential_speed, thermal_kelvin_field,
        arrhenius_multiplier, arrhenius_threshold, consumed_species_orders.T, net_molar_change,
        ablated_mixture_table, jnp.transpose(ablator_boundary_condition, (1, 0, 2)),
        holding_segment.reshape(1, ELEMS), intra_segment_position.reshape(1, ELEMS), shocked_level_bounds,
        jnp.asarray(strip_h), jnp.asarray(strip_l),
    )


def solution(mesh):
    in_specs = (
        P(None, "stream", None, "azim"),
        P("stream", None, "azim"),
        P("stream", None, "azim"),
        P("stream", None, "azim"),
        P(),
        P(),
        P(),
        P(),
        P(),
        P("stream", None, "azim"),
        P("stream"),
        P("stream"),
        P("stream", None),
    )
    out_specs = P(None, "stream", None, "azim")
    return jax.shard_map(local, mesh=mesh, in_specs=in_specs, out_specs=out_specs, check_vma=False)
```

```python
import functools
import math

import jax
import jax.numpy as jnp
import numpy as np
from jax import lax
from jax.experimental import pallas as pl
from jax.experimental.pallas import tpu as pltpu
from jax.sharding import PartitionSpec as P

STENCIL = (-1.0 / 60.0, 3.0 / 20.0, -0.75, 0.0, 0.75, -3.0 / 20.0, 1.0 / 60.0)
MESH = pl.DeviceIdType.MESH
HIGH = lax.Precision.HIGHEST
BF, F32 = jnp.bfloat16, jnp.float32

SP, CELLS, ROWS, PTS = 14, 8, 32, 128
REACT, ELEMS, BAND, GROUPS = 32, 256, 8, 8
NX, NZ, TILES = 4, 8, 32
PAD = ROWS - BAND
HALF = 16
CHUNKS = (((0, 4), (4, 8)), ((8, 11), (11, 14)))


def derivative_strip():
    points, modes = PTS * GROUPS, PTS * GROUPS // 2
    wave = np.arange(modes, dtype=np.float64)
    gain = np.where(3 * np.arange(modes) < 2 * modes, wave, 0.0)
    lag = np.arange(points)
    phase = (lag[:, None] * np.arange(modes)[None, :]) % points
    d = -2.0 / (points * modes) * (np.sin(phase * (2.0 * np.pi / points)) @ gain)
    strip = d[(lag[None, :] - np.arange(2 * PTS)[:, None]) % points].astype(np.float32)
    high = strip.astype(BF)
    low = (strip - high.astype(np.float32)).astype(BF)
    return high, low


def split(v):
    high = v.astype(BF)
    return high, (v - high.astype(F32)).astype(BF)


def dot(a, b):
    return jnp.dot(a, b, preferred_element_type=F32)


def dot3(ah, al, bh, bl):
    return dot(ah, bh) + dot(al, bh) + dot(ah, bl)


def spread(table, rows, cols):
    n, m = rows * HALF, cols * HALF
    left = (lax.broadcasted_iota(jnp.int32, (n, rows), 0) // HALF == lax.broadcasted_iota(jnp.int32, (n, rows), 1)).astype(F32).astype(BF)
    right = (lax.broadcasted_iota(jnp.int32, (cols, m), 1) // HALF == lax.broadcasted_iota(jnp.int32, (cols, m), 0)).astype(F32).astype(BF)
    same = lax.broadcasted_iota(jnp.int32, (n, m), 0) % HALF == lax.broadcasted_iota(jnp.int32, (n, m), 1) % HALF
    parts = []
    for part in split(table):
        wide = dot(dot(left, part).astype(BF), right)
        parts.append(jnp.where(same, wide, 0.0).astype(BF))
    return parts


def kernel(
    dens, axial, swirl, temp, mult_h, thr_h, cmat_h, nmat_h, tab_h, abl, seg_h, pos_h, bounds_h, strip_h, strip_l,
    out,
    mult, thr, cmat, nmat, tab, seg, pos, bounds, dens_v, axial_v, swirl_v, temp_v, abl_v, sh_v, sl_v, kch, kcl, knh, knl, w, m3r, m3l, xr1, xl1, xal, xar, y, zr,
    fs, fr, gs, zb, halo_l, halo_r, v_wall, loc, ss, rs,
):
    s = lax.axis_index("stream")
    a = lax.axis_index("azim")
    x, z = s // NZ, lax.rem(s, NZ)
    up, down = lax.rem(s + 1, TILES), lax.rem(s + TILES - 1, TILES)
    xr, xl, xo = lax.rem(x + 1, NX), lax.rem(x + NX - 1, NX), lax.rem(x + 2, NX)
    right, left = (xr * NZ + z, a), (xl * NZ + z, a)
    y_peer = [lax.rem(a + d, GROUPS) for d in range(1, GROUPS)]
    z_peer = [lax.rem(z + d, NZ) for d in range(1, NZ)]

    barrier = pltpu.get_barrier_semaphore()
    peers = [(up, a), (down, a), right, left]
    peers += [(s, p) for p in y_peer] + [(x * NZ + p, a) for p in z_peer]
    for p in peers:
        pl.semaphore_signal(barrier, inc=1, device_id=p, device_id_type=MESH)

    local = []
    for src, dst in (
        (seg_h, seg), (pos_h, pos), (abl, abl_v), (bounds_h, bounds), (dens, dens_v),
        (temp, temp_v), (axial, axial_v), (swirl, swirl_v), (mult_h, mult), (thr_h, thr), (tab_h, tab),
        (cmat_h, cmat), (nmat_h, nmat), (strip_h, sh_v), (strip_l, sl_v),
    ):
        c = pltpu.make_async_copy(src, dst, loc.at[len(local)])
        c.start()
        local.append(c)

    count = [0]

    def remote(src, dst, device):
        n = count[0]
        count[0] += 1
        return pltpu.make_async_remote_copy(
            src_ref=src, dst_ref=dst, send_sem=ss.at[n], recv_sem=rs.at[n], device_id=device, device_id_type=MESH
        )

    local[0].wait()
    local[1].wait()
    target = seg[...] * CELLS + pos[...]
    place = (lax.broadcasted_iota(jnp.int32, (TILES * CELLS, ELEMS), 0) == target).astype(F32).astype(BF)
    local[2].wait()
    for p in range(SP // 2):
        block = jnp.concatenate([abl_v[2 * p], abl_v[2 * p + 1]], axis=1)
        high, low = split(block)
        sums = dot(place, high) + dot(place, low)
        w[2 * p] = sums[:, :PTS]
        w[2 * p + 1] = sums[:, PTS:]

    local[3].wait()
    local[4].wait()
    start = jnp.minimum(bounds[0, 0], PAD)

    def gather(i, carry):
        for c in range(CELLS):
            fs[c, i] = dens_v[i, c, pl.ds(start, BAND), :]
        return carry

    lax.fori_loop(0, SP, gather, 0)
    pl.semaphore_wait(barrier, len(peers))

    def rows_of(block):
        return pl.ds(pl.multiple_of(block * NZ * CELLS, NZ * CELLS), NZ * CELLS)

    first, early, late = [], [], []
    for (r0, r1), (l0, l1) in CHUNKS:
        R, L = slice(r0, r1), slice(l0, l1)
        first.append([
            remote(w.at[R, rows_of(xo)], xr1.at[R], right),
            remote(w.at[L, rows_of(xo)], xl1.at[L], left),
        ])
        early.append([
            remote(w.at[L, rows_of(xr)], xal.at[L], right),
            remote(w.at[R, rows_of(xl)], xar.at[R], left),
        ])
        late.append([
            remote(m3r.at[R], xal.at[R], right),
            remote(m3l.at[L], xar.at[L], left),
        ])
    there, back = [], []
    for d in range(GROUPS - 1):
        there.append(remote(fs.at[y_peer[d]], fr.at[a], (s, y_peer[d])))
        back.append(remote(gs.at[y_peer[d]], zb.at[:, a, pl.ds(PAD, BAND)], (s, y_peer[d])))
    halo_up = remote(dens.at[:, CELLS - 3 : CELLS], halo_l, (up, a))
    halo_down = remote(dens.at[:, 0:3], halo_r, (down, a))
    z_sends = []
    for (r0, _), (_, l1) in CHUNKS:
        F = slice(r0, l1)
        z_sends.append([
            remote(y.at[F, pl.ds(pl.multiple_of(z_peer[d] * CELLS, CELLS), CELLS)], zr.at[d, F], (x * NZ + z_peer[d], a))
            for d in range(NZ - 1)
        ])

    for c in first[0] + early[0] + there:
        c.start()

    @pl.when(s < TILES - 1)
    def _():
        halo_up.start()

    @pl.when(s > 0)
    def _():
        halo_down.start()

    for c in first[1] + early[1]:
        c.start()

    fr[a] = fs[a]

    @pl.when(s == 0)
    def _():
        halo_l[...] = jnp.zeros_like(halo_l)

    @pl.when(s == TILES - 1)
    def _():
        halo_r[...] = jnp.zeros_like(halo_r)

    for c in local[5:]:
        c.wait()
    kch[...], kcl[...] = spread(jnp.transpose(cmat[...]), REACT, SP)
    knh[...], knl[...] = spread(nmat[...], SP, REACT)

    row = lax.broadcasted_iota(jnp.int32, (CELLS, ROWS, PTS), 1)
    in_band = (row >= bounds[0, 0]) & (row < bounds[0, 1])
    swirl_v[...] = jnp.where(in_band, swirl_v[...], 0.0)

    def clear(i, carry):
        zb[i, :, 0:PAD] = jnp.zeros((CELLS, PAD, PTS), F32)
        zb[i, :, PAD + BAND :] = jnp.zeros((CELLS, PAD, PTS), F32)
        return carry

    lax.fori_loop(0, SP, clear, 0)

    def chem(c, carry):
        block = dens_v[:, c]
        pair = jnp.concatenate(
            [block[:, :HALF].reshape(SP * HALF, PTS), block[:, HALF:].reshape(SP * HALF, PTS)], axis=1
        )
        high, low = split(pair)
        mixed = dot3(kch[...], kcl[...], high, low)
        minus = (-1.0 / math.log(2.0)) / temp_v[c]
        minus = jnp.concatenate([minus[:HALF], minus[HALF:]], axis=1)
        rate = jnp.concatenate([mult[q] * jnp.exp2(thr[q] * minus) for q in range(REACT)], axis=0)
        high, low = split(rate * mixed)
        made = dot3(knh[...], knl[...], high, low)
        out[:, c, 0:HALF] = made[:, :PTS].reshape(SP, HALF, PTS)
        out[:, c, HALF:] = made[:, PTS:].reshape(SP, HALF, PTS)
        return carry

    lax.fori_loop(0, 3, chem, 0)

    for k, ((r0, r1), (l0, l1)) in enumerate(CHUNKS):
        R, L = slice(r0, r1), slice(l0, l1)
        first[k][0].wait_recv()
        m3r[R] = w[R, rows_of(xr)] + xr1[R]
        late[k][0].start()
        first[k][1].wait_recv()
        m3l[L] = w[L, rows_of(xl)] + xl1[L]
        late[k][1].start()

    for c in there:
        c.wait_recv()
    lhs = jnp.concatenate(
        [
            jnp.concatenate([fr[2 * p].reshape(SP * BAND, PTS), fr[2 * p + 1].reshape(SP * BAND, PTS)], axis=1)
            for p in range(GROUPS // 2)
        ],
        axis=0,
    )
    high, low = split(lhs)
    n = SP * BAND
    shifted = [
        dot3(high, low, sh_v[:, 2 * PTS * c : 2 * PTS * (c + 1)], sl_v[:, 2 * PTS * c : 2 * PTS * (c + 1)])
        for c in range(GROUPS // 2)
    ]
    for q in range(GROUPS // 2):
        total = sum(shifted[(q - p) % 4][n * p : n * (p + 1)] for p in range(GROUPS // 2))
        gs[2 * q] = total[:, :PTS].reshape(SP, BAND, PTS)
        gs[2 * q + 1] = total[:, PTS:].reshape(SP, BAND, PTS)
    for c in back:
        c.start()
    zb[:, a, PAD : PAD + BAND] = gs[a]

    lax.fori_loop(3, 6, chem, 0)

    def finish_x(k):
        (r0, _), (_, l1) = CHUNKS[k]
        F = slice(r0, l1)
        for c in early[k] + late[k]:
            c.wait_recv()
        y[F] = w[F, rows_of(x)] + xal[F] + xar[F]
        for c in z_sends[k]:
            c.start()

    finish_x(0)
    lax.fori_loop(6, 8, chem, 0)
    finish_x(1)

    for c in back:
        c.wait_recv()

    def own(i, carry):
        f = dens_v[i]
        for c in range(CELLS):
            acc = None
            for j in (1, 2, 3):
                lo, hi = c - j >= 0, c + j < CELLS
                if lo and hi:
                    term = STENCIL[3 + j] * (f[c + j] - f[c - j])
                elif hi:
                    term = STENCIL[3 + j] * f[c + j]
                elif lo:
                    term = STENCIL[3 - j] * f[c - j]
                else:
                    continue
                acc = term if acc is None else acc + term
            around = zb[i, c, pl.ds(PAD - start, ROWS), :]
            out[i, c] = out[i, c] - axial_v[c] * acc - swirl_v[c] * around
        return carry

    lax.fori_loop(0, SP, own, 0)

    @pl.when(s > 0)
    def _():
        halo_up.wait_recv()

    @pl.when(s < TILES - 1)
    def _():
        halo_down.wait_recv()

    def ends(i, carry):
        before, after = halo_l[i], halo_r[i]
        for c in range(3):
            acc = sum(STENCIL[3 + j] * before[3 + c + j] for j in range(-3, -c))
            out[i, c] = out[i, c] - axial_v[c] * acc
            e = CELLS - 1 - c
            acc = sum(STENCIL[3 + j] * after[j - 1 - c] for j in range(c + 1, 4))
            out[i, e] = out[i, e] - axial_v[e] * acc
        return carry

    lax.fori_loop(0, SP, ends, 0)

    for k in range(len(CHUNKS)):
        for c in z_sends[k]:
            c.wait_recv()
    mine = pl.ds(pl.multiple_of(z * CELLS, CELLS), CELLS)
    for i in range(SP):
        v_wall[i] = y[i, mine] + sum(zr[d, i] for d in range(NZ - 1))
    for i in range(SP):
        wall = sum(tab[i, j] * v_wall[j] for j in range(SP))
        for c in range(CELLS):
            out[i, c, 0:1] = out[i, c, 0:1] + wall[c : c + 1]

    @pl.when(s < TILES - 1)
    def _():
        halo_up.wait_send()

    @pl.when(s > 0)
    def _():
        halo_down.wait_send()

    for group in first + early + late + z_sends + [there, back]:
        for c in group:
            c.wait_send()


def local(
    species_mass_density,
    axial_speed,
    circumferential_speed,
    thermal_kelvin_field,
    arrhenius_multiplier,
    arrhenius_threshold,
    consumed_species_orders,
    net_molar_change,
    ablated_mixture_table,
    ablator_boundary_condition,
    holding_segment,
    intra_segment_position,
    shocked_level_bounds,
):
    strip_h, strip_l = derivative_strip()
    far = pl.BlockSpec(memory_space=pltpu.HBM)
    near = pl.BlockSpec(memory_space=pltpu.VMEM)
    sm = lambda shape, dtype=F32: pltpu.SMEM(shape, dtype)
    vm = lambda shape, dtype=F32: pltpu.VMEM(shape, dtype)
    wide = NZ * CELLS
    copies = 6 * len(CHUNKS) + 2 * (GROUPS - 1) + 2 + len(CHUNKS) * (NZ - 1)
    keep = lambda v: pltpu.with_memory_space_constraint(v, pltpu.HBM)
    return pl.pallas_call(
        kernel,
        name="section",
        out_shape=jax.ShapeDtypeStruct((SP, CELLS, ROWS, PTS), F32),
        in_specs=[far] * 15,
        out_specs=near,
        scratch_shapes=[
            sm((REACT,)), sm((REACT,)), vm((SP, REACT)), vm((SP, REACT)), sm((SP, SP)),
            vm((1, ELEMS), jnp.int32), vm((1, ELEMS), jnp.int32), sm((1, 2), jnp.int32),
            vm((SP, CELLS, ROWS, PTS)), vm((CELLS, ROWS, PTS)), vm((CELLS, ROWS, PTS)), vm((CELLS, ROWS, PTS)),
            vm((SP, ELEMS, PTS)), vm((2 * PTS, GROUPS * PTS), BF), vm((2 * PTS, GROUPS * PTS), BF),
            vm((REACT * HALF, SP * HALF), BF), vm((REACT * HALF, SP * HALF), BF),
            vm((SP * HALF, REACT * HALF), BF), vm((SP * HALF, REACT * HALF), BF),
            vm((SP, TILES * CELLS, PTS)), vm((SP, wide, PTS)), vm((SP, wide, PTS)), vm((SP, wide, PTS)), vm((SP, wide, PTS)),
            vm((SP, wide, PTS)), vm((SP, wide, PTS)), vm((SP, wide, PTS)), vm((NZ - 1, SP, CELLS, PTS)),
            vm((GROUPS, SP, BAND, PTS)), vm((GROUPS, SP, BAND, PTS)), vm((GROUPS, SP, BAND, PTS)),
            vm((SP, CELLS, PAD + BAND + PAD, PTS)), vm((SP, 3, ROWS, PTS)), vm((SP, 3, ROWS, PTS)), vm((SP, CELLS, PTS)),
            pltpu.SemaphoreType.DMA((15,)), pltpu.SemaphoreType.DMA((copies,)), pltpu.SemaphoreType.DMA((copies,)),
        ],
        compiler_params=pltpu.CompilerParams(collective_id=0, has_side_effects=True, vmem_limit_bytes=28 << 20),
    )(*[
        keep(v)
        for v in (
            species_mass_density, axial_speed, circumferential_speed, thermal_kelvin_field,
            arrhenius_multiplier, arrhenius_threshold, consumed_species_orders.T, net_molar_change,
            ablated_mixture_table, jnp.transpose(ablator_boundary_condition, (1, 0, 2)),
            holding_segment.reshape(1, ELEMS), intra_segment_position.reshape(1, ELEMS), shocked_level_bounds,
            jnp.asarray(strip_h), jnp.asarray(strip_l),
        )
    ])


def solution(mesh):
    in_specs = (
        P(None, "stream", None, "azim"),
        P("stream", None, "azim"),
        P("stream", None, "azim"),
        P("stream", None, "azim"),
        P(),
        P(),
        P(),
        P(),
        P(),
        P("stream", None, "azim"),
        P("stream"),
        P("stream"),
        P("stream", None),
    )
    out_specs = P(None, "stream", None, "azim")
    return jax.shard_map(local, mesh=mesh, in_specs=in_specs, out_specs=out_specs, check_vma=False)
```

```python
import functools
import math

import jax
import jax.numpy as jnp
import numpy as np
from jax import lax
from jax.experimental import pallas as pl
from jax.experimental.pallas import tpu as pltpu
from jax.sharding import PartitionSpec as P

STENCIL = (-1.0 / 60.0, 3.0 / 20.0, -0.75, 0.0, 0.75, -3.0 / 20.0, 1.0 / 60.0)
MESH = pl.DeviceIdType.MESH
HIGH = lax.Precision.HIGHEST
BF, F32 = jnp.bfloat16, jnp.float32

SP, CELLS, ROWS, PTS = 14, 8, 32, 128
REACT, ELEMS, BAND, GROUPS = 32, 256, 8, 8
NX, NZ, TILES = 4, 8, 32
PAD = ROWS - BAND
HALF = 16
CHUNKS = (((0, 3), (3, 6)), ((6, 8), (8, 10)), ((10, 12), (12, 14)))
ALONG_Z, ALONG_X = (slice(0, 11),), (slice(11, 14),)


def derivative_strip():
    points, modes = PTS * GROUPS, PTS * GROUPS // 2
    wave = np.arange(modes, dtype=np.float64)
    gain = np.where(3 * np.arange(modes) < 2 * modes, wave, 0.0)
    lag = np.arange(points)
    phase = (lag[:, None] * np.arange(modes)[None, :]) % points
    d = -2.0 / (points * modes) * (np.sin(phase * (2.0 * np.pi / points)) @ gain)
    strip = d[(lag[None, :] - np.arange(2 * PTS)[:, None]) % points].astype(np.float32)
    high = strip.astype(BF)
    low = (strip - high.astype(np.float32)).astype(BF)
    return high, low


def split(v):
    high = v.astype(BF)
    return high, (v - high.astype(F32)).astype(BF)


def dot(a, b):
    return jnp.dot(a, b, preferred_element_type=F32)


def dot3(ah, al, bh, bl):
    return dot(ah, bh) + dot(al, bh) + dot(ah, bl)


def spread(table, rows, cols):
    n, m = rows * HALF, cols * HALF
    left = (lax.broadcasted_iota(jnp.int32, (n, rows), 0) // HALF == lax.broadcasted_iota(jnp.int32, (n, rows), 1)).astype(F32).astype(BF)
    right = (lax.broadcasted_iota(jnp.int32, (cols, m), 1) // HALF == lax.broadcasted_iota(jnp.int32, (cols, m), 0)).astype(F32).astype(BF)
    same = lax.broadcasted_iota(jnp.int32, (n, m), 0) % HALF == lax.broadcasted_iota(jnp.int32, (n, m), 1) % HALF
    parts = []
    for part in split(table):
        wide = dot(dot(left, part).astype(BF), right)
        parts.append(jnp.where(same, wide, 0.0).astype(BF))
    return parts


def kernel(
    dens, axial, swirl, temp, mult_h, thr_h, cmat_h, nmat_h, tab_h, abl, seg_h, pos_h, bounds_h, strip_h, strip_l,
    out,
    mult, thr, cmat, nmat, tab, seg, pos, bounds, dens_v, axial_v, swirl_v, temp_v, abl_v, sh_v, sl_v, kch, kcl, knh, knl, w, m3r, m3l, xr1, xl1, xal, xar, y, zr,
    fs, fr, gs, zb, halo_l, halo_r, turn_u, turn_d, v_wall, loc, ss, rs,
):
    s = lax.axis_index("stream")
    a = lax.axis_index("azim")
    x, z = s // NZ, lax.rem(s, NZ)
    up, down = lax.rem(s + 1, TILES), lax.rem(s + TILES - 1, TILES)
    xr, xl, xo = lax.rem(x + 1, NX), lax.rem(x + NX - 1, NX), lax.rem(x + 2, NX)
    right, left = (xr * NZ + z, a), (xl * NZ + z, a)
    y_peer = [lax.rem(a + d, GROUPS) for d in range(1, GROUPS)]
    z_peer = [lax.rem(z + d, NZ) for d in range(1, NZ)]

    barrier = pltpu.get_barrier_semaphore()
    peers = [(up, a), (down, a), right, left]
    peers += [(s, p) for p in y_peer] + [(x * NZ + p, a) for p in z_peer]
    for p in peers:
        pl.semaphore_signal(barrier, inc=1, device_id=p, device_id_type=MESH)

    local = []
    for src, dst in (
        (seg_h, seg), (pos_h, pos), (bounds_h, bounds), (dens, dens_v),
        (temp, temp_v), (axial, axial_v), (swirl, swirl_v), (mult_h, mult), (thr_h, thr), (tab_h, tab),
        (cmat_h, cmat), (nmat_h, nmat), (strip_h, sh_v), (strip_l, sl_v),
    ):
        c = pltpu.make_async_copy(src, dst, loc.at[len(local)])
        c.start()
        local.append(c)
    elements = []
    for (r0, _), (_, l1) in CHUNKS:
        c = pltpu.make_async_copy(abl.at[r0:l1], abl_v.at[r0:l1], loc.at[len(local) + len(elements)])
        c.start()
        elements.append(c)

    count = [0]

    def remote(src, dst, device):
        n = count[0]
        count[0] += 1
        return pltpu.make_async_remote_copy(
            src_ref=src, dst_ref=dst, send_sem=ss.at[n], recv_sem=rs.at[n], device_id=device, device_id_type=MESH
        )

    local[0].wait()
    local[1].wait()
    target = seg[...] * CELLS + pos[...]
    place = (lax.broadcasted_iota(jnp.int32, (TILES * CELLS, ELEMS), 0) == target).astype(F32).astype(BF)

    def place_chunk(k):
        (r0, _), (_, l1) = CHUNKS[k]
        elements[k].wait()
        for p in range(r0, l1, 2):
            high, low = split(jnp.concatenate([abl_v[p], abl_v[p + 1]], axis=1))
            sums = dot(place, high) + dot(place, low)
            w[p] = sums[:, :PTS]
            w[p + 1] = sums[:, PTS:]

    place_chunk(0)

    local[2].wait()
    local[3].wait()
    start = jnp.minimum(bounds[0, 0], PAD)

    def gather(i, carry):
        for c in range(CELLS):
            fs[c, i] = dens_v[i, c, pl.ds(start, BAND), :]
        return carry

    lax.fori_loop(0, SP, gather, 0)
    pl.semaphore_wait(barrier, len(peers))

    def rows_of(block):
        return pl.ds(pl.multiple_of(block * NZ * CELLS, NZ * CELLS), NZ * CELLS)

    first, early, late = [], [], []
    for (r0, r1), (l0, l1) in CHUNKS:
        R, L = slice(r0, r1), slice(l0, l1)
        first.append([
            remote(w.at[R, rows_of(xo)], xr1.at[R], right),
            remote(w.at[L, rows_of(xo)], xl1.at[L], left),
        ])
        early.append([
            remote(w.at[L, rows_of(xr)], xal.at[L], right),
            remote(w.at[R, rows_of(xl)], xar.at[R], left),
        ])
        late.append([
            remote(m3r.at[R], xal.at[R], right),
            remote(m3l.at[L], xar.at[L], left),
        ])
    there, back = [], []
    for d in range(GROUPS - 1):
        there.append(remote(fs.at[y_peer[d]], fr.at[a], (s, y_peer[d])))
        back.append(remote(gs.at[y_peer[d]], zb.at[:, a, pl.ds(PAD, BAND)], (s, y_peer[d])))
    low_z, high_z, not_first, not_last = z == 0, z == NZ - 1, x > 0, x < NX - 1
    to_low, to_high = (x * NZ, a), (x * NZ + NZ - 1, a)
    last, begin = slice(CELLS - 3, CELLS), slice(0, 3)
    plain, corner_zx, turn_zx, corner_xz, turn_xz = [], [], [], [], []
    for S in ALONG_Z + ALONG_X:
        plain.append((remote(dens.at[S, last], halo_l.at[S], (up, a)), z < NZ - 1, z > 0))
        plain.append((remote(dens.at[S, begin], halo_r.at[S], (down, a)), z > 0, z < NZ - 1))
    for S in ALONG_Z:
        corner_zx.append((remote(dens.at[S, last], turn_u.at[S], to_low), high_z & not_last, low_z & not_last))
        corner_zx.append((remote(dens.at[S, begin], turn_d.at[S], to_high), low_z & not_first, high_z & not_first))
        turn_zx.append((remote(turn_u.at[S], halo_l.at[S], right), low_z & not_last, low_z & not_first))
        turn_zx.append((remote(turn_d.at[S], halo_r.at[S], left), high_z & not_first, high_z & not_last))
    for S in ALONG_X:
        corner_xz.append((remote(dens.at[S, last], turn_u.at[S], right), high_z & not_last, high_z & not_first))
        corner_xz.append((remote(dens.at[S, begin], turn_d.at[S], left), low_z & not_first, low_z & not_last))
        turn_xz.append((remote(turn_u.at[S], halo_l.at[S], to_low), high_z & not_first, low_z & not_first))
        turn_xz.append((remote(turn_d.at[S], halo_r.at[S], to_high), low_z & not_last, high_z & not_last))

    def starts(group):
        for c, sent, _ in group:
            pl.when(sent)(c.start)

    def received(group):
        for c, _, got in group:
            pl.when(got)(c.wait_recv)

    def gone(group):
        for c, sent, _ in group:
            pl.when(sent)(c.wait_send)

    z_sends = []
    for (r0, _), (_, l1) in CHUNKS:
        F = slice(r0, l1)
        z_sends.append([
            remote(y.at[F, pl.ds(pl.multiple_of(z_peer[d] * CELLS, CELLS), CELLS)], zr.at[d, F], (x * NZ + z_peer[d], a))
            for d in range(NZ - 1)
        ])

    for c in first[0] + there:
        c.start()
    starts(plain + corner_zx)
    place_chunk(1)
    for c in first[1]:
        c.start()
    place_chunk(2)
    for c in first[2] + early[0]:
        c.start()

    fr[a] = fs[a]

    @pl.when(s == 0)
    def _():
        halo_l[...] = jnp.zeros_like(halo_l)

    @pl.when(s == TILES - 1)
    def _():
        halo_r[...] = jnp.zeros_like(halo_r)

    for c in local[4:]:
        c.wait()
    kch[...], kcl[...] = spread(jnp.transpose(cmat[...]), REACT, SP)
    knh[...], knl[...] = spread(nmat[...], SP, REACT)

    row = lax.broadcasted_iota(jnp.int32, (CELLS, ROWS, PTS), 1)
    in_band = (row >= bounds[0, 0]) & (row < bounds[0, 1])
    swirl_v[...] = jnp.where(in_band, swirl_v[...], 0.0)

    def clear(i, carry):
        zb[i, :, 0:PAD] = jnp.zeros((CELLS, PAD, PTS), F32)
        zb[i, :, PAD + BAND :] = jnp.zeros((CELLS, PAD, PTS), F32)
        return carry

    lax.fori_loop(0, SP, clear, 0)

    def chem(c, carry):
        block = dens_v[:, c]
        pair = jnp.concatenate(
            [block[:, :HALF].reshape(SP * HALF, PTS), block[:, HALF:].reshape(SP * HALF, PTS)], axis=1
        )
        high, low = split(pair)
        mixed = dot3(kch[...], kcl[...], high, low)
        minus = (-1.0 / math.log(2.0)) / temp_v[c]
        minus = jnp.concatenate([minus[:HALF], minus[HALF:]], axis=1)
        rate = jnp.concatenate([mult[q] * jnp.exp2(thr[q] * minus) for q in range(REACT)], axis=0)
        high, low = split(rate * mixed)
        made = dot3(knh[...], knl[...], high, low)
        out[:, c, 0:HALF] = made[:, :PTS].reshape(SP, HALF, PTS)
        out[:, c, HALF:] = made[:, PTS:].reshape(SP, HALF, PTS)
        return carry

    def pass_on(k):
        (r0, r1), (l0, l1) = CHUNKS[k]
        R, L = slice(r0, r1), slice(l0, l1)
        first[k][0].wait_recv()
        m3r[R] = w[R, rows_of(xr)] + xr1[R]
        late[k][0].start()
        first[k][1].wait_recv()
        m3l[L] = w[L, rows_of(xl)] + xl1[L]
        late[k][1].start()

    lax.fori_loop(0, 2, chem, 0)
    pass_on(0)
    for c in early[1]:
        c.start()
    lax.fori_loop(2, 3, chem, 0)
    pass_on(1)
    for c in early[2]:
        c.start()
    lax.fori_loop(3, 4, chem, 0)

    for c in there:
        c.wait_recv()
    lhs = jnp.concatenate(
        [
            jnp.concatenate([fr[2 * p].reshape(SP * BAND, PTS), fr[2 * p + 1].reshape(SP * BAND, PTS)], axis=1)
            for p in range(GROUPS // 2)
        ],
        axis=0,
    )
    high, low = split(lhs)
    n = SP * BAND
    shifted = [
        dot3(high, low, sh_v[:, 2 * PTS * c : 2 * PTS * (c + 1)], sl_v[:, 2 * PTS * c : 2 * PTS * (c + 1)])
        for c in range(GROUPS // 2)
    ]
    for q in range(GROUPS // 2):
        total = sum(shifted[(q - p) % 4][n * p : n * (p + 1)] for p in range(GROUPS // 2))
        gs[2 * q] = total[:, :PTS].reshape(SP, BAND, PTS)
        gs[2 * q + 1] = total[:, PTS:].reshape(SP, BAND, PTS)
    for c in back:
        c.start()
    zb[:, a, PAD : PAD + BAND] = gs[a]

    pass_on(2)
    starts(corner_xz)
    lax.fori_loop(4, 8, chem, 0)
    received(corner_zx)
    starts(turn_zx)

    def finish_x(k):
        (r0, _), (_, l1) = CHUNKS[k]
        F = slice(r0, l1)
        for c in early[k] + late[k]:
            c.wait_recv()
        y[F] = w[F, rows_of(x)] + xal[F] + xar[F]
        for c in z_sends[k]:
            c.start()

    finish_x(0)
    finish_x(1)
    for c in back:
        c.wait_recv()

    def own(i, carry):
        f = dens_v[i]
        for c in range(CELLS):
            acc = None
            for j in (1, 2, 3):
                lo, hi = c - j >= 0, c + j < CELLS
                if lo and hi:
                    term = STENCIL[3 + j] * (f[c + j] - f[c - j])
                elif hi:
                    term = STENCIL[3 + j] * f[c + j]
                elif lo:
                    term = STENCIL[3 - j] * f[c - j]
                else:
                    continue
                acc = term if acc is None else acc + term
            around = zb[i, c, pl.ds(PAD - start, ROWS), :]
            out[i, c] = out[i, c] - axial_v[c] * acc - swirl_v[c] * around
        return carry

    lax.fori_loop(0, SP, own, 0)

    finish_x(2)
    for turned, sent in zip(corner_xz, turn_xz):
        received([turned])
        starts([sent])
    received(plain + turn_zx + turn_xz)

    def ends(i, carry):
        before, after = halo_l[i], halo_r[i]
        for c in range(3):
            acc = sum(STENCIL[3 + j] * before[3 + c + j] for j in range(-3, -c))
            out[i, c] = out[i, c] - axial_v[c] * acc
            e = CELLS - 1 - c
            acc = sum(STENCIL[3 + j] * after[j - 1 - c] for j in range(c + 1, 4))
            out[i, e] = out[i, e] - axial_v[e] * acc
        return carry

    lax.fori_loop(0, SP, ends, 0)

    for k in range(len(CHUNKS)):
        for c in z_sends[k]:
            c.wait_recv()
    mine = pl.ds(pl.multiple_of(z * CELLS, CELLS), CELLS)
    for i in range(SP):
        v_wall[i] = y[i, mine] + sum(zr[d, i] for d in range(NZ - 1))
    for i in range(SP):
        wall = sum(tab[i, j] * v_wall[j] for j in range(SP))
        for c in range(CELLS):
            out[i, c, 0:1] = out[i, c, 0:1] + wall[c : c + 1]

    gone(plain + corner_zx + turn_zx + corner_xz + turn_xz)
    for group in first + early + late + z_sends + [there, back]:
        for c in group:
            c.wait_send()


def local(
    species_mass_density,
    axial_speed,
    circumferential_speed,
    thermal_kelvin_field,
    arrhenius_multiplier,
    arrhenius_threshold,
    consumed_species_orders,
    net_molar_change,
    ablated_mixture_table,
    ablator_boundary_condition,
    holding_segment,
    intra_segment_position,
    shocked_level_bounds,
):
    strip_h, strip_l = derivative_strip()
    far = pl.BlockSpec(memory_space=pltpu.HBM)
    near = pl.BlockSpec(memory_space=pltpu.VMEM)
    sm = lambda shape, dtype=F32: pltpu.SMEM(shape, dtype)
    vm = lambda shape, dtype=F32: pltpu.VMEM(shape, dtype)
    wide = NZ * CELLS
    copies = 6 * len(CHUNKS) + 2 * (GROUPS - 1) + 6 * len(ALONG_Z + ALONG_X) + len(CHUNKS) * (NZ - 1)
    keep = lambda v: pltpu.with_memory_space_constraint(v, pltpu.HBM)
    return pl.pallas_call(
        kernel,
        name="section",
        out_shape=jax.ShapeDtypeStruct((SP, CELLS, ROWS, PTS), F32),
        in_specs=[far] * 15,
        out_specs=near,
        scratch_shapes=[
            sm((REACT,)), sm((REACT,)), vm((SP, REACT)), vm((SP, REACT)), sm((SP, SP)),
            vm((1, ELEMS), jnp.int32), vm((1, ELEMS), jnp.int32), sm((1, 2), jnp.int32),
            vm((SP, CELLS, ROWS, PTS)), vm((CELLS, ROWS, PTS)), vm((CELLS, ROWS, PTS)), vm((CELLS, ROWS, PTS)),
            vm((SP, ELEMS, PTS)), vm((2 * PTS, GROUPS * PTS), BF), vm((2 * PTS, GROUPS * PTS), BF),
            vm((REACT * HALF, SP * HALF), BF), vm((REACT * HALF, SP * HALF), BF),
            vm((SP * HALF, REACT * HALF), BF), vm((SP * HALF, REACT * HALF), BF),
            vm((SP, TILES * CELLS, PTS)), vm((SP, wide, PTS)), vm((SP, wide, PTS)), vm((SP, wide, PTS)), vm((SP, wide, PTS)),
            vm((SP, wide, PTS)), vm((SP, wide, PTS)), vm((SP, wide, PTS)), vm((NZ - 1, SP, CELLS, PTS)),
            vm((GROUPS, SP, BAND, PTS)), vm((GROUPS, SP, BAND, PTS)), vm((GROUPS, SP, BAND, PTS)),
            vm((SP, CELLS, PAD + BAND + PAD, PTS)), vm((SP, 3, ROWS, PTS)), vm((SP, 3, ROWS, PTS)), vm((SP, 3, ROWS, PTS)), vm((SP, 3, ROWS, PTS)), vm((SP, CELLS, PTS)),
            pltpu.SemaphoreType.DMA((14 + len(CHUNKS),)), pltpu.SemaphoreType.DMA((copies,)), pltpu.SemaphoreType.DMA((copies,)),
        ],
        compiler_params=pltpu.CompilerParams(collective_id=0, has_side_effects=True, vmem_limit_bytes=28 << 20),
    )(*[
        keep(v)
        for v in (
            species_mass_density, axial_speed, circumferential_speed, thermal_kelvin_field,
            arrhenius_multiplier, arrhenius_threshold, consumed_species_orders.T, net_molar_change,
            ablated_mixture_table, jnp.transpose(ablator_boundary_condition, (1, 0, 2)),
            holding_segment.reshape(1, ELEMS), intra_segment_position.reshape(1, ELEMS), shocked_level_bounds,
            jnp.asarray(strip_h), jnp.asarray(strip_l),
        )
    ])


def solution(mesh):
    in_specs = (
        P(None, "stream", None, "azim"),
        P("stream", None, "azim"),
        P("stream", None, "azim"),
        P("stream", None, "azim"),
        P(),
        P(),
        P(),
        P(),
        P(),
        P("stream", None, "azim"),
        P("stream"),
        P("stream"),
        P("stream", None),
    )
    out_specs = P(None, "stream", None, "azim")
    return jax.shard_map(local, mesh=mesh, in_specs=in_specs, out_specs=out_specs, check_vma=False)
```

```python
import functools
import math

import jax
import jax.numpy as jnp
import numpy as np
from jax import lax
from jax.experimental import pallas as pl
from jax.experimental.pallas import tpu as pltpu
from jax.sharding import PartitionSpec as P

STENCIL = (-1.0 / 60.0, 3.0 / 20.0, -0.75, 0.0, 0.75, -3.0 / 20.0, 1.0 / 60.0)
MESH = pl.DeviceIdType.MESH
HIGH = lax.Precision.HIGHEST
BF, F32 = jnp.bfloat16, jnp.float32

SP, CELLS, ROWS, PTS = 14, 8, 32, 128
REACT, ELEMS, BAND, GROUPS = 32, 256, 8, 8
NX, NZ, TILES = 4, 8, 32
PAD = ROWS - BAND
HALF = 16
CHUNKS = (((0, 3), (3, 6)), ((6, 9), (9, 12)), ((12, 13), (13, 14)))
ALONG_Z, ALONG_X = (slice(0, 4), slice(4, 8), slice(8, 11)), (slice(11, 13), slice(13, 14))
AHEAD = 4


def derivative_strip():
    points, modes = PTS * GROUPS, PTS * GROUPS // 2
    wave = np.arange(modes, dtype=np.float64)
    gain = np.where(3 * np.arange(modes) < 2 * modes, wave, 0.0)
    lag = np.arange(points)
    phase = (lag[:, None] * np.arange(modes)[None, :]) % points
    d = -2.0 / (points * modes) * (np.sin(phase * (2.0 * np.pi / points)) @ gain)
    strip = d[(lag[None, :] - np.arange(2 * PTS)[:, None]) % points].astype(np.float32)
    high = strip.astype(BF)
    low = (strip - high.astype(np.float32)).astype(BF)
    return high, low


def split(v):
    high = v.astype(BF)
    return high, (v - high.astype(F32)).astype(BF)


def dot(a, b):
    return jnp.dot(a, b, preferred_element_type=F32)


def dot3(ah, al, bh, bl):
    return dot(ah, bh) + dot(al, bh) + dot(ah, bl)


def spread(table, rows, cols):
    n, m = rows * HALF, cols * HALF
    left = (lax.broadcasted_iota(jnp.int32, (n, rows), 0) // HALF == lax.broadcasted_iota(jnp.int32, (n, rows), 1)).astype(F32).astype(BF)
    right = (lax.broadcasted_iota(jnp.int32, (cols, m), 1) // HALF == lax.broadcasted_iota(jnp.int32, (cols, m), 0)).astype(F32).astype(BF)
    same = lax.broadcasted_iota(jnp.int32, (n, m), 0) % HALF == lax.broadcasted_iota(jnp.int32, (n, m), 1) % HALF
    parts = []
    for part in split(table):
        wide = dot(dot(left, part).astype(BF), right)
        parts.append(jnp.where(same, wide, 0.0).astype(BF))
    return parts


def kernel(
    dens, axial, swirl, temp, mult_h, thr_h, cmat_h, nmat_h, tab_h, abl, seg_h, pos_h, bounds_h, strip_h, strip_l,
    out,
    mult, thr, cmat, nmat, tab, seg, pos, bounds, dens_v, axial_v, swirl_v, temp_v, abl_v, sh_v, sl_v, kch, kcl, knh, knl, w, m3r, m3l, xr1, xl1, xal, xar, y, zr, far3, far4, two,
    fs, fr, gs, zb, halo_l, halo_r, turn_u, turn_d, v_wall, loc, ss, rs,
):
    s = lax.axis_index("stream")
    a = lax.axis_index("azim")
    x, z = s // NZ, lax.rem(s, NZ)
    up, down = lax.rem(s + 1, TILES), lax.rem(s + TILES - 1, TILES)
    xr, xl, xo = lax.rem(x + 1, NX), lax.rem(x + NX - 1, NX), lax.rem(x + 2, NX)
    right, left = (xr * NZ + z, a), (xl * NZ + z, a)
    y_peer = [lax.rem(a + d, GROUPS) for d in range(1, GROUPS)]
    z_peer = [lax.rem(z + d, NZ) for d in range(1, NZ)]

    barrier = pltpu.get_barrier_semaphore()
    peers = [(up, a), (down, a), right, left]
    peers += [(s, p) for p in y_peer] + [(x * NZ + p, a) for p in z_peer]
    for p in peers:
        pl.semaphore_signal(barrier, inc=1, device_id=p, device_id_type=MESH)

    local = []
    for src, dst in (
        (seg_h, seg), (pos_h, pos), (bounds_h, bounds), (dens, dens_v),
        (temp, temp_v), (axial, axial_v), (swirl, swirl_v), (mult_h, mult), (thr_h, thr), (tab_h, tab),
        (cmat_h, cmat), (nmat_h, nmat), (strip_h, sh_v), (strip_l, sl_v),
    ):
        c = pltpu.make_async_copy(src, dst, loc.at[len(local)])
        c.start()
        local.append(c)
    elements = []
    for (r0, _), (_, l1) in CHUNKS:
        c = pltpu.make_async_copy(abl.at[r0:l1], abl_v.at[r0:l1], loc.at[len(local) + len(elements)])
        c.start()
        elements.append(c)

    count = [0]

    def remote(src, dst, device):
        n = count[0]
        count[0] += 1
        return pltpu.make_async_remote_copy(
            src_ref=src, dst_ref=dst, send_sem=ss.at[n], recv_sem=rs.at[n], device_id=device, device_id_type=MESH
        )

    local[0].wait()
    local[1].wait()
    target = seg[...] * CELLS + pos[...]
    place = (lax.broadcasted_iota(jnp.int32, (TILES * CELLS, ELEMS), 0) == target).astype(F32).astype(BF)

    def place_chunk(k):
        (r0, _), (_, l1) = CHUNKS[k]
        elements[k].wait()
        for p in range(r0, l1, 2):
            high, low = split(jnp.concatenate([abl_v[p], abl_v[p + 1]], axis=1))
            sums = dot(place, high) + dot(place, low)
            w[p] = sums[:, :PTS]
            w[p + 1] = sums[:, PTS:]

    place_chunk(0)

    pl.semaphore_wait(barrier, len(peers))

    def rows_of(block):
        return pl.ds(pl.multiple_of(block * NZ * CELLS, NZ * CELLS), NZ * CELLS)

    first, early, late = [], [], []
    for (r0, r1), (l0, l1) in CHUNKS:
        R, L = slice(r0, r1), slice(l0, l1)
        first.append([
            remote(w.at[R, rows_of(xo)], xr1.at[R], right),
            remote(w.at[L, rows_of(xo)], xl1.at[L], left),
        ])
        early.append([
            remote(w.at[L, rows_of(xr)], xal.at[L], right),
            remote(w.at[R, rows_of(xl)], xar.at[R], left),
        ])
        late.append([
            remote(m3r.at[R], xal.at[R], right),
            remote(m3l.at[L], xar.at[L], left),
        ])
    there, back = [], []
    for d in range(GROUPS - 1):
        there.append(remote(fs.at[y_peer[d]], fr.at[a], (s, y_peer[d])))
        back.append(remote(gs.at[y_peer[d]], zb.at[:, a, pl.ds(PAD, BAND)], (s, y_peer[d])))
    low_z, high_z, not_first, not_last = z == 0, z == NZ - 1, x > 0, x < NX - 1
    to_low, to_high = (x * NZ, a), (x * NZ + NZ - 1, a)
    last, begin = slice(CELLS - 3, CELLS), slice(0, 3)
    plain, corner_zx, turn_zx, corner_xz, turn_xz = [], [], [], [], []
    for S in ALONG_Z + ALONG_X:
        plain.append((remote(dens.at[S, last], halo_l.at[S], (up, a)), z < NZ - 1, z > 0))
        plain.append((remote(dens.at[S, begin], halo_r.at[S], (down, a)), z > 0, z < NZ - 1))
    for S in ALONG_Z:
        corner_zx.append((remote(dens.at[S, last], turn_u.at[S], to_low), high_z & not_last, low_z & not_last))
        corner_zx.append((remote(dens.at[S, begin], turn_d.at[S], to_high), low_z & not_first, high_z & not_first))
        turn_zx.append((remote(turn_u.at[S], halo_l.at[S], right), low_z & not_last, low_z & not_first))
        turn_zx.append((remote(turn_d.at[S], halo_r.at[S], left), high_z & not_first, high_z & not_last))
    for S in ALONG_X:
        corner_xz.append((remote(dens.at[S, last], turn_u.at[S], right), high_z & not_last, high_z & not_first))
        corner_xz.append((remote(dens.at[S, begin], turn_d.at[S], left), low_z & not_first, low_z & not_last))
        turn_xz.append((remote(turn_u.at[S], halo_l.at[S], to_low), high_z & not_first, low_z & not_first))
        turn_xz.append((remote(turn_d.at[S], halo_r.at[S], to_high), low_z & not_last, high_z & not_last))

    def starts(group):
        for c, sent, _ in group:
            pl.when(sent)(c.start)

    def received(group):
        for c, _, got in group:
            pl.when(got)(c.wait_recv)

    def gone(group):
        for c, sent, _ in group:
            pl.when(sent)(c.wait_send)

    def z_to(d):
        return (x * NZ + lax.rem(z + d + NZ, NZ), a)

    def block_z(d):
        return pl.ds(pl.multiple_of(lax.rem(z + d + NZ, NZ) * CELLS, CELLS), CELLS)

    z_far, z_near, z_two = [], [], []
    for (r0, r1), (l0, l1) in CHUNKS:
        F, R, L = slice(r0, l1), slice(r0, r1), slice(l0, l1)
        z_far.append([
            remote(y.at[F, block_z(3)], far3.at[0, F], z_to(1)),
            remote(y.at[F, block_z(-3)], far3.at[1, F], z_to(-1)),
            remote(y.at[R, block_z(4)], far4.at[0, R], z_to(2)),
            remote(y.at[L, block_z(4)], far4.at[1, L], z_to(-2)),
        ])
        z_near.append([
            remote(y.at[F, block_z(1)], zr.at[0, F], z_to(1)),
            remote(y.at[F, block_z(-1)], zr.at[1, F], z_to(-1)),
        ])
        z_two.append([
            remote(two.at[0, F], zr.at[2, F], z_to(2)),
            remote(two.at[1, F], zr.at[3, F], z_to(-2)),
        ])

    for c in first[0]:
        c.start()
    starts(corner_zx + plain[: 2 * AHEAD])

    local[2].wait()
    local[3].wait()
    start = jnp.minimum(bounds[0, 0], PAD)

    def gather(i, carry):
        for c in range(CELLS):
            fs[c, i] = dens_v[i, c, pl.ds(start, BAND), :]
        return carry

    lax.fori_loop(0, SP, gather, 0)
    for c in there:
        c.start()
    place_chunk(1)
    for c in first[1]:
        c.start()
    place_chunk(2)
    for c in first[2] + early[0]:
        c.start()

    fr[a] = fs[a]

    @pl.when(s == 0)
    def _():
        halo_l[...] = jnp.zeros_like(halo_l)

    @pl.when(s == TILES - 1)
    def _():
        halo_r[...] = jnp.zeros_like(halo_r)

    for c in local[4:]:
        c.wait()
    kch[...], kcl[...] = spread(jnp.transpose(cmat[...]), REACT, SP)
    knh[...], knl[...] = spread(nmat[...], SP, REACT)

    row = lax.broadcasted_iota(jnp.int32, (CELLS, ROWS, PTS), 1)
    in_band = (row >= bounds[0, 0]) & (row < bounds[0, 1])
    swirl_v[...] = jnp.where(in_band, swirl_v[...], 0.0)

    def clear(i, carry):
        zb[i, :, 0:PAD] = jnp.zeros((CELLS, PAD, PTS), F32)
        zb[i, :, PAD + BAND :] = jnp.zeros((CELLS, PAD, PTS), F32)
        return carry

    lax.fori_loop(0, SP, clear, 0)

    def chem(c, carry):
        block = dens_v[:, c]
        pair = jnp.concatenate(
            [block[:, :HALF].reshape(SP * HALF, PTS), block[:, HALF:].reshape(SP * HALF, PTS)], axis=1
        )
        high, low = split(pair)
        mixed = dot3(kch[...], kcl[...], high, low)
        minus = (-1.0 / math.log(2.0)) / temp_v[c]
        minus = jnp.concatenate([minus[:HALF], minus[HALF:]], axis=1)
        rate = jnp.concatenate([mult[q] * jnp.exp2(thr[q] * minus) for q in range(REACT)], axis=0)
        high, low = split(rate * mixed)
        made = dot3(knh[...], knl[...], high, low)
        out[:, c, 0:HALF] = made[:, :PTS].reshape(SP, HALF, PTS)
        out[:, c, HALF:] = made[:, PTS:].reshape(SP, HALF, PTS)
        return carry

    def pass_on(k):
        (r0, r1), (l0, l1) = CHUNKS[k]
        R, L = slice(r0, r1), slice(l0, l1)
        first[k][0].wait_recv()
        m3r[R] = w[R, rows_of(xr)] + xr1[R]
        late[k][0].start()
        first[k][1].wait_recv()
        m3l[L] = w[L, rows_of(xl)] + xl1[L]
        late[k][1].start()

    lax.fori_loop(0, 2, chem, 0)
    pass_on(0)
    for c in early[1]:
        c.start()
    lax.fori_loop(2, 3, chem, 0)
    pass_on(1)
    for c in early[2]:
        c.start()
    lax.fori_loop(3, 4, chem, 0)

    for c in there:
        c.wait_recv()
    lhs = jnp.concatenate(
        [
            jnp.concatenate([fr[2 * p].reshape(SP * BAND, PTS), fr[2 * p + 1].reshape(SP * BAND, PTS)], axis=1)
            for p in range(GROUPS // 2)
        ],
        axis=0,
    )
    high, low = split(lhs)
    n = SP * BAND
    shifted = [
        dot3(high, low, sh_v[:, 2 * PTS * c : 2 * PTS * (c + 1)], sl_v[:, 2 * PTS * c : 2 * PTS * (c + 1)])
        for c in range(GROUPS // 2)
    ]
    for q in range(GROUPS // 2):
        total = sum(shifted[(q - p) % 4][n * p : n * (p + 1)] for p in range(GROUPS // 2))
        gs[2 * q] = total[:, :PTS].reshape(SP, BAND, PTS)
        gs[2 * q + 1] = total[:, PTS:].reshape(SP, BAND, PTS)
    for c in back:
        c.start()
    zb[:, a, PAD : PAD + BAND] = gs[a]

    pass_on(2)
    starts(corner_xz)

    def turn(pieces, onward, k):
        for c, sent in zip(pieces[2 * k : 2 * k + 2], onward[2 * k : 2 * k + 2]):
            received([c])
            starts([sent])

    turn(corner_zx, turn_zx, 0)
    lax.fori_loop(4, 6, chem, 0)
    turn(corner_zx, turn_zx, 1)
    lax.fori_loop(6, 8, chem, 0)

    def finish_x(k):
        (r0, _), (_, l1) = CHUNKS[k]
        F = slice(r0, l1)
        for c in early[k] + late[k]:
            c.wait_recv()
        y[F] = w[F, rows_of(x)] + xal[F] + xar[F]
        for c in z_far[k] + z_near[k]:
            c.start()

    def finish_z(k):
        (r0, r1), (l0, l1) = CHUNKS[k]
        for c in z_far[k]:
            c.wait_recv()
        two[0, r0:r1] = y[r0:r1, block_z(2)] + far3[0, r0:r1] + far4[0, r0:r1]
        two[0, l0:l1] = y[l0:l1, block_z(2)] + far3[0, l0:l1]
        two[1, r0:r1] = y[r0:r1, block_z(-2)] + far3[1, r0:r1]
        two[1, l0:l1] = y[l0:l1, block_z(-2)] + far3[1, l0:l1] + far4[1, l0:l1]
        for c in z_two[k]:
            c.start()

    finish_x(0)
    for k in range(2, len(ALONG_Z)):
        turn(corner_zx, turn_zx, k)
    starts(plain[2 * AHEAD :])
    finish_x(1)
    finish_z(0)
    for c in back:
        c.wait_recv()

    def own(i, carry):
        f = dens_v[i]
        for c in range(CELLS):
            acc = None
            for j in (1, 2, 3):
                lo, hi = c - j >= 0, c + j < CELLS
                if lo and hi:
                    term = STENCIL[3 + j] * (f[c + j] - f[c - j])
                elif hi:
                    term = STENCIL[3 + j] * f[c + j]
                elif lo:
                    term = STENCIL[3 - j] * f[c - j]
                else:
                    continue
                acc = term if acc is None else acc + term
            around = zb[i, c, pl.ds(PAD - start, ROWS), :]
            out[i, c] = out[i, c] - axial_v[c] * acc - swirl_v[c] * around
        return carry

    lax.fori_loop(0, SP, own, 0)

    finish_x(2)
    finish_z(1)
    finish_z(2)
    for k in range(len(ALONG_X)):
        turn(corner_xz, turn_xz, k)
    received(plain + turn_zx + turn_xz)

    def ends(i, carry):
        before, after = halo_l[i], halo_r[i]
        for c in range(3):
            acc = sum(STENCIL[3 + j] * before[3 + c + j] for j in range(-3, -c))
            out[i, c] = out[i, c] - axial_v[c] * acc
            e = CELLS - 1 - c
            acc = sum(STENCIL[3 + j] * after[j - 1 - c] for j in range(c + 1, 4))
            out[i, e] = out[i, e] - axial_v[e] * acc
        return carry

    lax.fori_loop(0, SP, ends, 0)

    for k in range(len(CHUNKS)):
        for c in z_near[k] + z_two[k]:
            c.wait_recv()
    mine = pl.ds(pl.multiple_of(z * CELLS, CELLS), CELLS)
    for i in range(SP):
        v_wall[i] = y[i, mine] + sum(zr[d, i] for d in range(4))
    for i in range(SP):
        wall = sum(tab[i, j] * v_wall[j] for j in range(SP))
        for c in range(CELLS):
            out[i, c, 0:1] = out[i, c, 0:1] + wall[c : c + 1]

    gone(plain + corner_zx + turn_zx + corner_xz + turn_xz)
    for group in first + early + late + z_far + z_near + z_two + [there, back]:
        for c in group:
            c.wait_send()


def local(
    species_mass_density,
    axial_speed,
    circumferential_speed,
    thermal_kelvin_field,
    arrhenius_multiplier,
    arrhenius_threshold,
    consumed_species_orders,
    net_molar_change,
    ablated_mixture_table,
    ablator_boundary_condition,
    holding_segment,
    intra_segment_position,
    shocked_level_bounds,
):
    strip_h, strip_l = derivative_strip()
    far = pl.BlockSpec(memory_space=pltpu.HBM)
    near = pl.BlockSpec(memory_space=pltpu.VMEM)
    sm = lambda shape, dtype=F32: pltpu.SMEM(shape, dtype)
    vm = lambda shape, dtype=F32: pltpu.VMEM(shape, dtype)
    wide = NZ * CELLS
    copies = 6 * len(CHUNKS) + 2 * (GROUPS - 1) + 6 * len(ALONG_Z + ALONG_X) + 8 * len(CHUNKS)
    keep = lambda v: pltpu.with_memory_space_constraint(v, pltpu.HBM)
    return pl.pallas_call(
        kernel,
        name="section",
        out_shape=jax.ShapeDtypeStruct((SP, CELLS, ROWS, PTS), F32),
        in_specs=[far] * 15,
        out_specs=near,
        scratch_shapes=[
            sm((REACT,)), sm((REACT,)), vm((SP, REACT)), vm((SP, REACT)), sm((SP, SP)),
            vm((1, ELEMS), jnp.int32), vm((1, ELEMS), jnp.int32), sm((1, 2), jnp.int32),
            vm((SP, CELLS, ROWS, PTS)), vm((CELLS, ROWS, PTS)), vm((CELLS, ROWS, PTS)), vm((CELLS, ROWS, PTS)),
            vm((SP, ELEMS, PTS)), vm((2 * PTS, GROUPS * PTS), BF), vm((2 * PTS, GROUPS * PTS), BF),
            vm((REACT * HALF, SP * HALF), BF), vm((REACT * HALF, SP * HALF), BF),
            vm((SP * HALF, REACT * HALF), BF), vm((SP * HALF, REACT * HALF), BF),
            vm((SP, TILES * CELLS, PTS)), vm((SP, wide, PTS)), vm((SP, wide, PTS)), vm((SP, wide, PTS)), vm((SP, wide, PTS)),
            vm((SP, wide, PTS)), vm((SP, wide, PTS)), vm((SP, wide, PTS)), vm((4, SP, CELLS, PTS)), vm((2, SP, CELLS, PTS)), vm((2, SP, CELLS, PTS)), vm((2, SP, CELLS, PTS)),
            vm((GROUPS, SP, BAND, PTS)), vm((GROUPS, SP, BAND, PTS)), vm((GROUPS, SP, BAND, PTS)),
            vm((SP, CELLS, PAD + BAND + PAD, PTS)), vm((SP, 3, ROWS, PTS)), vm((SP, 3, ROWS, PTS)), vm((SP, 3, ROWS, PTS)), vm((SP, 3, ROWS, PTS)), vm((SP, CELLS, PTS)),
            pltpu.SemaphoreType.DMA((14 + len(CHUNKS),)), pltpu.SemaphoreType.DMA((copies,)), pltpu.SemaphoreType.DMA((copies,)),
        ],
        compiler_params=pltpu.CompilerParams(collective_id=0, has_side_effects=True, vmem_limit_bytes=28 << 20),
    )(*[
        keep(v)
        for v in (
            species_mass_density, axial_speed, circumferential_speed, thermal_kelvin_field,
            arrhenius_multiplier, arrhenius_threshold, consumed_species_orders.T, net_molar_change,
            ablated_mixture_table, jnp.transpose(ablator_boundary_condition, (1, 0, 2)),
            holding_segment.reshape(1, ELEMS), intra_segment_position.reshape(1, ELEMS), shocked_level_bounds,
            jnp.asarray(strip_h), jnp.asarray(strip_l),
        )
    ])


def solution(mesh):
    in_specs = (
        P(None, "stream", None, "azim"),
        P("stream", None, "azim"),
        P("stream", None, "azim"),
        P("stream", None, "azim"),
        P(),
        P(),
        P(),
        P(),
        P(),
        P("stream", None, "azim"),
        P("stream"),
        P("stream"),
        P("stream", None),
    )
    out_specs = P(None, "stream", None, "azim")
    return jax.shard_map(local, mesh=mesh, in_specs=in_specs, out_specs=out_specs, check_vma=False)
```

```python
import functools
import math

import jax
import jax.numpy as jnp
import numpy as np
from jax import lax
from jax.experimental import pallas as pl
from jax.experimental.pallas import tpu as pltpu
from jax.sharding import PartitionSpec as P

STENCIL = (-1.0 / 60.0, 3.0 / 20.0, -0.75, 0.0, 0.75, -3.0 / 20.0, 1.0 / 60.0)
MESH = pl.DeviceIdType.MESH
HIGH = lax.Precision.HIGHEST
BF, F32 = jnp.bfloat16, jnp.float32

SP, CELLS, ROWS, PTS = 14, 8, 32, 128
REACT, ELEMS, BAND, GROUPS = 32, 256, 8, 8
NX, NZ, TILES = 4, 8, 32
PAD = ROWS - BAND
HALF = 16
CHUNKS = (((0, 3), (3, 6)), ((6, 9), (9, 12)), ((12, 13), (13, 14)))
ALONG_Z, ALONG_X = (slice(0, 4), slice(4, 8), slice(8, 11)), (slice(11, 12), slice(12, 13), slice(13, 14))
EARLY_PARTS = 2
AHEAD = 5


def derivative_strip():
    points, modes = PTS * GROUPS, PTS * GROUPS // 2
    wave = np.arange(modes, dtype=np.float64)
    gain = np.where(3 * np.arange(modes) < 2 * modes, wave, 0.0)
    lag = np.arange(points)
    phase = (lag[:, None] * np.arange(modes)[None, :]) % points
    d = -2.0 / (points * modes) * (np.sin(phase * (2.0 * np.pi / points)) @ gain)
    strip = d[(lag[None, :] - np.arange(2 * PTS)[:, None]) % points].astype(np.float32)
    high = strip.astype(BF)
    low = (strip - high.astype(np.float32)).astype(BF)
    return high, low


def split(v):
    high = v.astype(BF)
    return high, (v - high.astype(F32)).astype(BF)


def dot(a, b):
    return jnp.dot(a, b, preferred_element_type=F32)


def dot3(ah, al, bh, bl):
    return dot(ah, bh) + dot(al, bh) + dot(ah, bl)


def spread(table, rows, cols):
    n, m = rows * HALF, cols * HALF
    left = (lax.broadcasted_iota(jnp.int32, (n, rows), 0) // HALF == lax.broadcasted_iota(jnp.int32, (n, rows), 1)).astype(F32).astype(BF)
    right = (lax.broadcasted_iota(jnp.int32, (cols, m), 1) // HALF == lax.broadcasted_iota(jnp.int32, (cols, m), 0)).astype(F32).astype(BF)
    same = lax.broadcasted_iota(jnp.int32, (n, m), 0) % HALF == lax.broadcasted_iota(jnp.int32, (n, m), 1) % HALF
    parts = []
    for part in split(table):
        wide = dot(dot(left, part).astype(BF), right)
        parts.append(jnp.where(same, wide, 0.0).astype(BF))
    return parts


def kernel(
    dens, axial, swirl, temp, mult_h, thr_h, cmat_h, nmat_h, tab_h, abl, seg_h, pos_h, bounds_h, strip_h, strip_l,
    out,
    mult, thr, cmat, nmat, tab, seg, pos, bounds, dens_v, axial_v, swirl_v, temp_v, abl_v, sh_v, sl_v, kch, kcl, knh, knl, w, m3r, m3l, xr1, xl1, xal, xar, y, zr, far3, far4, two,
    fs, fr, gs, zb, halo_l, halo_r, turn_u, turn_d, v_wall, loc, ss, rs,
):
    s = lax.axis_index("stream")
    a = lax.axis_index("azim")
    x, z = s // NZ, lax.rem(s, NZ)
    up, down = lax.rem(s + 1, TILES), lax.rem(s + TILES - 1, TILES)
    xr, xl, xo = lax.rem(x + 1, NX), lax.rem(x + NX - 1, NX), lax.rem(x + 2, NX)
    right, left = (xr * NZ + z, a), (xl * NZ + z, a)
    y_peer = [lax.rem(a + d, GROUPS) for d in range(1, GROUPS)]
    z_peer = [lax.rem(z + d, NZ) for d in range(1, NZ)]

    barrier = pltpu.get_barrier_semaphore()
    peers = [(up, a), (down, a), right, left]
    peers += [(s, p) for p in y_peer] + [(x * NZ + p, a) for p in z_peer]
    for p in peers:
        pl.semaphore_signal(barrier, inc=1, device_id=p, device_id_type=MESH)

    local = []
    for src, dst in (
        (seg_h, seg), (pos_h, pos), (bounds_h, bounds), (dens, dens_v),
        (temp, temp_v), (axial, axial_v), (swirl, swirl_v), (mult_h, mult), (thr_h, thr), (tab_h, tab),
        (cmat_h, cmat), (nmat_h, nmat), (strip_h, sh_v), (strip_l, sl_v),
    ):
        c = pltpu.make_async_copy(src, dst, loc.at[len(local)])
        c.start()
        local.append(c)
    elements = []
    for (r0, _), (_, l1) in CHUNKS:
        c = pltpu.make_async_copy(abl.at[r0:l1], abl_v.at[r0:l1], loc.at[len(local) + len(elements)])
        c.start()
        elements.append(c)

    count = [0]

    def remote(src, dst, device):
        n = count[0]
        count[0] += 1
        return pltpu.make_async_remote_copy(
            src_ref=src, dst_ref=dst, send_sem=ss.at[n], recv_sem=rs.at[n], device_id=device, device_id_type=MESH
        )

    local[0].wait()
    local[1].wait()
    target = seg[...] * CELLS + pos[...]
    place = (lax.broadcasted_iota(jnp.int32, (TILES * CELLS, ELEMS), 0) == target).astype(F32).astype(BF)

    def place_chunk(k):
        (r0, _), (_, l1) = CHUNKS[k]
        elements[k].wait()
        for p in range(r0, l1, 2):
            high, low = split(jnp.concatenate([abl_v[p], abl_v[p + 1]], axis=1))
            sums = dot(place, high) + dot(place, low)
            w[p] = sums[:, :PTS]
            w[p + 1] = sums[:, PTS:]

    place_chunk(0)

    pl.semaphore_wait(barrier, len(peers))

    def rows_of(block):
        return pl.ds(pl.multiple_of(block * NZ * CELLS, NZ * CELLS), NZ * CELLS)

    first, early, late = [], [], []
    for (r0, r1), (l0, l1) in CHUNKS:
        R, L = slice(r0, r1), slice(l0, l1)
        first.append([
            remote(w.at[R, rows_of(xo)], xr1.at[R], right),
            remote(w.at[L, rows_of(xo)], xl1.at[L], left),
        ])
        early.append([
            remote(w.at[L, rows_of(xr)], xal.at[L], right),
            remote(w.at[R, rows_of(xl)], xar.at[R], left),
        ])
        late.append([
            remote(m3r.at[R], xal.at[R], right),
            remote(m3l.at[L], xar.at[L], left),
        ])
    there, back = [], []
    for d in range(GROUPS - 1):
        there.append(remote(fs.at[y_peer[d]], fr.at[a], (s, y_peer[d])))
        back.append(remote(gs.at[y_peer[d]], zb.at[:, a, pl.ds(PAD, BAND)], (s, y_peer[d])))
    low_z, high_z, not_first, not_last = z == 0, z == NZ - 1, x > 0, x < NX - 1
    to_low, to_high = (x * NZ, a), (x * NZ + NZ - 1, a)
    last, begin = slice(CELLS - 3, CELLS), slice(0, 3)
    plain, corner_zx, turn_zx, corner_xz, turn_xz = [], [], [], [], []
    for S in ALONG_Z + ALONG_X:
        plain.append((remote(dens.at[S, last], halo_l.at[S], (up, a)), z < NZ - 1, z > 0))
        plain.append((remote(dens.at[S, begin], halo_r.at[S], (down, a)), z > 0, z < NZ - 1))
    for S in ALONG_Z:
        corner_zx.append((remote(dens.at[S, last], turn_u.at[S], to_low), high_z & not_last, low_z & not_last))
        corner_zx.append((remote(dens.at[S, begin], turn_d.at[S], to_high), low_z & not_first, high_z & not_first))
        turn_zx.append((remote(turn_u.at[S], halo_l.at[S], right), low_z & not_last, low_z & not_first))
        turn_zx.append((remote(turn_d.at[S], halo_r.at[S], left), high_z & not_first, high_z & not_last))
    for S in ALONG_X:
        corner_xz.append((remote(dens.at[S, last], turn_u.at[S], right), high_z & not_last, high_z & not_first))
        corner_xz.append((remote(dens.at[S, begin], turn_d.at[S], left), low_z & not_first, low_z & not_last))
        turn_xz.append((remote(turn_u.at[S], halo_l.at[S], to_low), high_z & not_first, low_z & not_first))
        turn_xz.append((remote(turn_d.at[S], halo_r.at[S], to_high), low_z & not_last, high_z & not_last))

    def starts(group):
        for c, sent, _ in group:
            pl.when(sent)(c.start)

    def received(group):
        for c, _, got in group:
            pl.when(got)(c.wait_recv)

    def gone(group):
        for c, sent, _ in group:
            pl.when(sent)(c.wait_send)

    def z_to(d):
        return (x * NZ + lax.rem(z + d + NZ, NZ), a)

    def block_z(d):
        return pl.ds(pl.multiple_of(lax.rem(z + d + NZ, NZ) * CELLS, CELLS), CELLS)

    z_far, z_near, z_two = [], [], []
    for (r0, r1), (l0, l1) in CHUNKS:
        F, R, L = slice(r0, l1), slice(r0, r1), slice(l0, l1)
        z_far.append([
            remote(y.at[F, block_z(3)], far3.at[0, F], z_to(1)),
            remote(y.at[F, block_z(-3)], far3.at[1, F], z_to(-1)),
            remote(y.at[R, block_z(4)], far4.at[0, R], z_to(2)),
            remote(y.at[L, block_z(4)], far4.at[1, L], z_to(-2)),
        ])
        z_near.append([
            remote(y.at[F, block_z(1)], zr.at[0, F], z_to(1)),
            remote(y.at[F, block_z(-1)], zr.at[1, F], z_to(-1)),
        ])
        z_two.append([
            remote(two.at[0, F], zr.at[2, F], z_to(2)),
            remote(two.at[1, F], zr.at[3, F], z_to(-2)),
        ])

    for c in first[0]:
        c.start()
    starts(corner_zx + plain[: 2 * AHEAD])

    local[2].wait()
    local[3].wait()
    start = jnp.minimum(bounds[0, 0], PAD)

    def gather(i, carry):
        for c in range(CELLS):
            fs[c, i] = dens_v[i, c, pl.ds(start, BAND), :]
        return carry

    lax.fori_loop(0, SP, gather, 0)
    for c in there:
        c.start()
    place_chunk(1)
    for c in first[1]:
        c.start()
    place_chunk(2)
    for c in first[2] + early[0]:
        c.start()

    fr[a] = fs[a]

    @pl.when(s == 0)
    def _():
        halo_l[...] = jnp.zeros_like(halo_l)

    @pl.when(s == TILES - 1)
    def _():
        halo_r[...] = jnp.zeros_like(halo_r)

    for c in local[4:]:
        c.wait()
    kch[...], kcl[...] = spread(jnp.transpose(cmat[...]), REACT, SP)
    knh[...], knl[...] = spread(nmat[...], SP, REACT)

    row = lax.broadcasted_iota(jnp.int32, (CELLS, ROWS, PTS), 1)
    in_band = (row >= bounds[0, 0]) & (row < bounds[0, 1])
    swirl_v[...] = jnp.where(in_band, swirl_v[...], 0.0)

    def clear(i, carry):
        zb[i, :, 0:PAD] = jnp.zeros((CELLS, PAD, PTS), F32)
        zb[i, :, PAD + BAND :] = jnp.zeros((CELLS, PAD, PTS), F32)
        return carry

    lax.fori_loop(0, SP, clear, 0)

    def chem(c, carry):
        block = dens_v[:, c]
        pair = jnp.concatenate(
            [block[:, :HALF].reshape(SP * HALF, PTS), block[:, HALF:].reshape(SP * HALF, PTS)], axis=1
        )
        high, low = split(pair)
        mixed = dot3(kch[...], kcl[...], high, low)
        minus = (-1.0 / math.log(2.0)) / temp_v[c]
        minus = jnp.concatenate([minus[:HALF], minus[HALF:]], axis=1)
        rate = jnp.concatenate([mult[q] * jnp.exp2(thr[q] * minus) for q in range(REACT)], axis=0)
        high, low = split(rate * mixed)
        made = dot3(knh[...], knl[...], high, low)
        out[:, c, 0:HALF] = made[:, :PTS].reshape(SP, HALF, PTS)
        out[:, c, HALF:] = made[:, PTS:].reshape(SP, HALF, PTS)
        return carry

    def pass_on(k):
        (r0, r1), (l0, l1) = CHUNKS[k]
        R, L = slice(r0, r1), slice(l0, l1)
        first[k][0].wait_recv()
        m3r[R] = w[R, rows_of(xr)] + xr1[R]
        late[k][0].start()
        first[k][1].wait_recv()
        m3l[L] = w[L, rows_of(xl)] + xl1[L]
        late[k][1].start()

    lax.fori_loop(0, 2, chem, 0)
    pass_on(0)
    for c in early[1]:
        c.start()
    lax.fori_loop(2, 3, chem, 0)
    pass_on(1)
    for c in early[2]:
        c.start()
    lax.fori_loop(3, 4, chem, 0)

    for c in there:
        c.wait_recv()
    lhs = jnp.concatenate(
        [
            jnp.concatenate([fr[2 * p].reshape(SP * BAND, PTS), fr[2 * p + 1].reshape(SP * BAND, PTS)], axis=1)
            for p in range(GROUPS // 2)
        ],
        axis=0,
    )
    high, low = split(lhs)
    n = SP * BAND
    shifted = [
        dot3(high, low, sh_v[:, 2 * PTS * c : 2 * PTS * (c + 1)], sl_v[:, 2 * PTS * c : 2 * PTS * (c + 1)])
        for c in range(GROUPS // 2)
    ]
    for q in range(GROUPS // 2):
        total = sum(shifted[(q - p) % 4][n * p : n * (p + 1)] for p in range(GROUPS // 2))
        gs[2 * q] = total[:, :PTS].reshape(SP, BAND, PTS)
        gs[2 * q + 1] = total[:, PTS:].reshape(SP, BAND, PTS)
    for c in back:
        c.start()
    zb[:, a, PAD : PAD + BAND] = gs[a]

    pass_on(2)
    starts(corner_xz)

    def turn(pieces, onward, k):
        for c, sent in zip(pieces[2 * k : 2 * k + 2], onward[2 * k : 2 * k + 2]):
            received([c])
            starts([sent])

    turn(corner_zx, turn_zx, 0)
    lax.fori_loop(4, 6, chem, 0)
    turn(corner_zx, turn_zx, 1)
    lax.fori_loop(6, 8, chem, 0)

    def finish_x(k):
        (r0, _), (_, l1) = CHUNKS[k]
        F = slice(r0, l1)
        for c in early[k] + late[k]:
            c.wait_recv()
        y[F] = w[F, rows_of(x)] + xal[F] + xar[F]
        for c in z_far[k] + z_near[k]:
            c.start()

    def finish_z(k):
        (r0, r1), (l0, l1) = CHUNKS[k]
        for c in z_far[k]:
            c.wait_recv()
        two[0, r0:r1] = y[r0:r1, block_z(2)] + far3[0, r0:r1] + far4[0, r0:r1]
        two[0, l0:l1] = y[l0:l1, block_z(2)] + far3[0, l0:l1]
        two[1, r0:r1] = y[r0:r1, block_z(-2)] + far3[1, r0:r1]
        two[1, l0:l1] = y[l0:l1, block_z(-2)] + far3[1, l0:l1] + far4[1, l0:l1]
        for c in z_two[k]:
            c.start()

    finish_x(0)
    for k in range(2, len(ALONG_Z)):
        turn(corner_zx, turn_zx, k)
    starts(plain[2 * AHEAD :])
    finish_x(1)
    finish_z(0)
    for c in back:
        c.wait_recv()

    def own(i, carry):
        f = dens_v[i]
        for c in range(CELLS):
            acc = None
            for j in (1, 2, 3):
                lo, hi = c - j >= 0, c + j < CELLS
                if lo and hi:
                    term = STENCIL[3 + j] * (f[c + j] - f[c - j])
                elif hi:
                    term = STENCIL[3 + j] * f[c + j]
                elif lo:
                    term = STENCIL[3 - j] * f[c - j]
                else:
                    continue
                acc = term if acc is None else acc + term
            around = zb[i, c, pl.ds(PAD - start, ROWS), :]
            out[i, c] = out[i, c] - axial_v[c] * acc - swirl_v[c] * around
        return carry

    lax.fori_loop(0, SP, own, 0)

    finish_x(2)
    finish_z(1)
    finish_z(2)
    for k in range(len(ALONG_X)):
        turn(corner_xz, turn_xz, k)

    def ends(i, carry):
        before, after = halo_l[i], halo_r[i]
        for c in range(3):
            acc = sum(STENCIL[3 + j] * before[3 + c + j] for j in range(-3, -c))
            out[i, c] = out[i, c] - axial_v[c] * acc
            e = CELLS - 1 - c
            acc = sum(STENCIL[3 + j] * after[j - 1 - c] for j in range(c + 1, 4))
            out[i, e] = out[i, e] - axial_v[e] * acc
        return carry

    def halo_part(k):
        onward = (turn_zx + turn_xz)[2 * k : 2 * k + 2]
        received(plain[2 * k : 2 * k + 2] + onward)
        S = (ALONG_Z + ALONG_X)[k]
        lax.fori_loop(S.start, S.stop, ends, 0)

    for k in range(EARLY_PARTS):
        halo_part(k)

    for k in range(len(CHUNKS)):
        for c in z_near[k] + z_two[k]:
            c.wait_recv()
    mine = pl.ds(pl.multiple_of(z * CELLS, CELLS), CELLS)
    for i in range(SP):
        v_wall[i] = y[i, mine] + sum(zr[d, i] for d in range(4))
    for i in range(SP):
        wall = sum(tab[i, j] * v_wall[j] for j in range(SP))
        for c in range(CELLS):
            out[i, c, 0:1] = out[i, c, 0:1] + wall[c : c + 1]

    for k in range(EARLY_PARTS, len(ALONG_Z + ALONG_X)):
        halo_part(k)


    gone(plain + corner_zx + turn_zx + corner_xz + turn_xz)
    for group in first + early + late + z_far + z_near + z_two + [there, back]:
        for c in group:
            c.wait_send()


def local(
    species_mass_density,
    axial_speed,
    circumferential_speed,
    thermal_kelvin_field,
    arrhenius_multiplier,
    arrhenius_threshold,
    consumed_species_orders,
    net_molar_change,
    ablated_mixture_table,
    ablator_boundary_condition,
    holding_segment,
    intra_segment_position,
    shocked_level_bounds,
):
    strip_h, strip_l = derivative_strip()
    far = pl.BlockSpec(memory_space=pltpu.HBM)
    near = pl.BlockSpec(memory_space=pltpu.VMEM)
    sm = lambda shape, dtype=F32: pltpu.SMEM(shape, dtype)
    vm = lambda shape, dtype=F32: pltpu.VMEM(shape, dtype)
    wide = NZ * CELLS
    copies = 6 * len(CHUNKS) + 2 * (GROUPS - 1) + 6 * len(ALONG_Z + ALONG_X) + 8 * len(CHUNKS)
    keep = lambda v: pltpu.with_memory_space_constraint(v, pltpu.HBM)
    return pl.pallas_call(
        kernel,
        name="section",
        out_shape=jax.ShapeDtypeStruct((SP, CELLS, ROWS, PTS), F32),
        in_specs=[far] * 15,
        out_specs=near,
        scratch_shapes=[
            sm((REACT,)), sm((REACT,)), vm((SP, REACT)), vm((SP, REACT)), sm((SP, SP)),
            vm((1, ELEMS), jnp.int32), vm((1, ELEMS), jnp.int32), sm((1, 2), jnp.int32),
            vm((SP, CELLS, ROWS, PTS)), vm((CELLS, ROWS, PTS)), vm((CELLS, ROWS, PTS)), vm((CELLS, ROWS, PTS)),
            vm((SP, ELEMS, PTS)), vm((2 * PTS, GROUPS * PTS), BF), vm((2 * PTS, GROUPS * PTS), BF),
            vm((REACT * HALF, SP * HALF), BF), vm((REACT * HALF, SP * HALF), BF),
            vm((SP * HALF, REACT * HALF), BF), vm((SP * HALF, REACT * HALF), BF),
            vm((SP, TILES * CELLS, PTS)), vm((SP, wide, PTS)), vm((SP, wide, PTS)), vm((SP, wide, PTS)), vm((SP, wide, PTS)),
            vm((SP, wide, PTS)), vm((SP, wide, PTS)), vm((SP, wide, PTS)), vm((4, SP, CELLS, PTS)), vm((2, SP, CELLS, PTS)), vm((2, SP, CELLS, PTS)), vm((2, SP, CELLS, PTS)),
            vm((GROUPS, SP, BAND, PTS)), vm((GROUPS, SP, BAND, PTS)), vm((GROUPS, SP, BAND, PTS)),
            vm((SP, CELLS, PAD + BAND + PAD, PTS)), vm((SP, 3, ROWS, PTS)), vm((SP, 3, ROWS, PTS)), vm((SP, 3, ROWS, PTS)), vm((SP, 3, ROWS, PTS)), vm((SP, CELLS, PTS)),
            pltpu.SemaphoreType.DMA((14 + len(CHUNKS),)), pltpu.SemaphoreType.DMA((copies,)), pltpu.SemaphoreType.DMA((copies,)),
        ],
        compiler_params=pltpu.CompilerParams(collective_id=0, has_side_effects=True, vmem_limit_bytes=28 << 20),
    )(*[
        keep(v)
        for v in (
            species_mass_density, axial_speed, circumferential_speed, thermal_kelvin_field,
            arrhenius_multiplier, arrhenius_threshold, consumed_species_orders.T, net_molar_change,
            ablated_mixture_table, jnp.transpose(ablator_boundary_condition, (1, 0, 2)),
            holding_segment.reshape(1, ELEMS), intra_segment_position.reshape(1, ELEMS), shocked_level_bounds,
            jnp.asarray(strip_h), jnp.asarray(strip_l),
        )
    ])


def solution(mesh):
    in_specs = (
        P(None, "stream", None, "azim"),
        P("stream", None, "azim"),
        P("stream", None, "azim"),
        P("stream", None, "azim"),
        P(),
        P(),
        P(),
        P(),
        P(),
        P("stream", None, "azim"),
        P("stream"),
        P("stream"),
        P("stream", None),
    )
    out_specs = P(None, "stream", None, "azim")
    return jax.shard_map(local, mesh=mesh, in_specs=in_specs, out_specs=out_specs, check_vma=False)
```
